512 devices in a mesh: acq: 32 (over y_hi, x, core), band: 16 (over z, y_lo).
Axes of the slice: x: 4, y: 8 (y_hi: 4, y_lo: 2; y = y_hi * 2 + y_lo), z: 8, core: 2. Of those that a mesh axis runs over, the one named last changes fastest.
Arguments:
- images: bfloat16 [2, 192, 176, 704], P(None, 'acq', 'band'), may hold values from -121 to 121
- pixel_shift: int32 [192, 2], P('acq'), may hold values from -3 to 3
- fraction_index: int32 [192, 2], P('acq'), may hold values from 0 to 15
Outputs:
- linked: float32 [2, 192, 16, 64], P(None, 'acq', 'band')
The draws below stay inside these ranges and needn't reach their ends.
All inputs are finite; a program needn't handle non-finite values.
Results may differ from the reference program's by a relative error of at most 0.0043.
Values may be sent and summed in bfloat16 or wider, within the bound.
A program may use at most 64 MiB of HBM per device.

```python
import jax
import jax.numpy as jnp
from jax import lax

ACQ = 192
PATCH = 11
QUANT = 16
HALO = 7
ITERS = 4
PROWS = 16
ROWS = 176
COLS = 704


def draw_images(key, part):
    keys = jax.random.split(jax.random.fold_in(key, 17), 3)
    amplitude = jnp.exp(jax.random.uniform(keys[0], (1, ACQ, 1, 1), jnp.float32) * jnp.log(10.0))
    texture = jnp.exp(jax.random.uniform(keys[1], (1, 1, ROWS, COLS), jnp.float32, -0.7, 0.7))
    values = jnp.clip(jax.random.normal(keys[2], (2, ACQ, ROWS, COLS), jnp.float32), -6.0, 6.0)
    return (values * amplitude * texture).astype(jnp.bfloat16)


def plant(values, own_key, low, high):
    index_at = [jax.random.randint(jax.random.fold_in(own_key, axis), (), 0, length) for axis, length in enumerate(values.shape)]
    widest = values.shape.index(max(values.shape))
    beside = index_at[:widest] + [(index_at[widest] + 1) % values.shape[widest]] + index_at[widest + 1:]
    return values.at[tuple(index_at)].set(low).at[tuple(beside)].set(high)


def setup_inputs(seed: int = 0) -> dict:
    seeds = jax.random.split(jax.random.key(seed), 4)
    images = draw_images(jax.random.fold_in(seeds[3], 71), 0)
    pixel_shift = plant(jax.random.randint(seeds[1], (ACQ, 2), -3, 4), jax.random.fold_in(seeds[1], 1), -3, 3).astype(jnp.int32)
    fraction_index = plant(jax.random.randint(seeds[2], (ACQ, 2), 0, QUANT), jax.random.fold_in(seeds[2], 1), 0, QUANT - 1).astype(jnp.int32)
    return {"images": images, "pixel_shift": pixel_shift, "fraction_index": fraction_index}


def tap_table():
    fraction = jnp.arange(QUANT, dtype=jnp.float32)[:, None] / QUANT
    offsets = jnp.arange(8, dtype=jnp.float32)[None, :]
    where_at = offsets - 3.0 - fraction
    raw_taps = jnp.sinc(where_at) * (0.5 + 0.5 * jnp.cos(jnp.pi * where_at / 4.0))
    return raw_taps / lax.optimization_barrier(jnp.sum(raw_taps, axis=1, keepdims=True))

def lookup_taps(fractions, tap_rows):
    onehot = (fractions[:, None] == jnp.arange(QUANT, dtype=jnp.int32)[None, :]).astype(jnp.float32)
    return lax.optimization_barrier(jnp.sum(onehot[:, :, None] * tap_rows[None, :, :], axis=1))

def resample_one(image, row_shift, col_shift, row_taps, col_taps, out_rows, out_cols):
    across = jnp.zeros((2, out_rows + 2 * HALO, out_cols), jnp.float32)
    for tap in range(8):
        start = (col_shift + (HALO + tap - 3)).astype(jnp.int32)
        piece = lax.dynamic_slice_in_dim(image, start, out_cols, 2)
        across = across + col_taps[tap] * piece.astype(jnp.float32)
    result = jnp.zeros((2, out_rows, out_cols), jnp.float32)
    for tap in range(8):
        start = (row_shift + (HALO + tap - 3)).astype(jnp.int32)
        result = result + row_taps[tap] * lax.dynamic_slice_in_dim(across, start, out_rows, 1)
    return result.astype(jnp.bfloat16)

def phase_link(block):
    acq_count = block.shape[1]
    patch_count = block.shape[3] // PATCH
    stacked = block.reshape(2, acq_count, PATCH, patch_count, PATCH)
    stacked = jnp.transpose(stacked, (3, 0, 1, 2, 4)).reshape(patch_count, 2 * acq_count, PATCH * PATCH)
    stacked = stacked.astype(jnp.float32)
    gram = jnp.einsum('pik,pjk->pij', stacked, stacked, precision=lax.Precision.HIGHEST)
    real_part = gram[:, :acq_count, :acq_count] + gram[:, acq_count:, acq_count:]
    imag_part = gram[:, acq_count:, :acq_count] - gram[:, :acq_count, acq_count:]
    power = jnp.diagonal(real_part, axis1=1, axis2=2) / (PATCH * PATCH) + 1e-06
    scaling = lax.rsqrt(power)
    factor = scaling[:, :, None] * scaling[:, None, :] / (PATCH * PATCH)
    gamma = jnp.stack([real_part * factor, imag_part * factor], axis=1)
    vectors = jnp.stack([jnp.ones((patch_count, acq_count), jnp.float32), jnp.zeros((patch_count, acq_count), jnp.float32)], axis=1)
    high = lax.Precision.HIGHEST
    for step in range(ITERS):
        products = jnp.einsum('pcab,pdb->pcda', gamma, vectors, precision=high)
        new_re = products[:, 0, 0] - products[:, 1, 1]
        new_im = products[:, 0, 1] + products[:, 1, 0]
        total = (lax.optimization_barrier(jnp.sum(new_re * new_re, axis=1)) + lax.optimization_barrier(jnp.sum(new_im * new_im, axis=1))) / (2 * acq_count)
        inverse = lax.rsqrt(total + 1e-06)[:, None]
        vectors = jnp.stack([new_re * inverse, new_im * inverse], axis=1)
    return jnp.transpose(vectors, (1, 2, 0))

def reference(images, pixel_shift, fraction_index):
    tap_rows = tap_table()
    padded = jnp.pad(images, ((0, 0), (0, 0), (HALO, HALO), (HALO, HALO)))
    rows_all = images.shape[2]
    cols_all = images.shape[3]

    def resample_acq(index):
        image = lax.dynamic_index_in_dim(padded, index, 1, keepdims=False)
        shifts = lax.dynamic_index_in_dim(pixel_shift, index, 0, keepdims=False)
        fractions = lax.dynamic_index_in_dim(fraction_index, index, 0, keepdims=False)
        taps_now = lookup_taps(fractions, tap_rows)
        return resample_one(image, shifts[0], shifts[1], taps_now[0], taps_now[1], rows_all, cols_all)
    resampled = lax.map(resample_acq, jnp.arange(ACQ, dtype=jnp.int32))

    def patch_row(index):
        rows_block = lax.dynamic_slice_in_dim(resampled, (index * PATCH).astype(jnp.int32), PATCH, 2)
        return phase_link(jnp.transpose(rows_block, (1, 0, 2, 3)))
    linked = lax.map(patch_row, jnp.arange(PROWS, dtype=jnp.int32))
    return jnp.transpose(linked, (1, 2, 0, 3))
```

```python
import functools

import jax
import jax.numpy as jnp
import numpy as np
from jax import lax
from jax.experimental import pallas as pl
from jax.experimental.pallas import tpu as pltpu
from jax.sharding import PartitionSpec as P

PATCH = 11
QUANT = 16
HALO = 7
ITERS = 4
MESH = pl.DeviceIdType.MESH

ROWS = 11
LANES = 768
BLOCK = 22
RING = 256
ABOVE = 6
BELOW = 7
TOP = 80
BOTTOM = 96
LOCAL = 192
EDGE = TOP + BOTTOM


def tap_table():
    fraction = np.arange(QUANT, dtype=np.float64)[:, None] / QUANT
    where_at = np.arange(8, dtype=np.float64)[None, :] - 3.0 - fraction
    raw_taps = np.sinc(where_at) * (0.5 + 0.5 * np.cos(np.pi * where_at / 4.0))
    return (raw_taps / raw_taps.sum(axis=1, keepdims=True)).astype(np.float32)


def index_rows(acqs):
    rows = np.full((16, 256), -1, np.float32)
    for c in range(2):
        for a in range(acqs):
            for i in range(ROWS):
                k = (c * acqs + a) * 16 + i
                rows[2, k], rows[3, k], rows[4, k] = a, i, c
            for t in range(ABOVE):
                m = (c * acqs + a) * ABOVE + t
                rows[0, (c * acqs + a) * 16 + ROWS - ABOVE + t] = m
                rows[5, m], rows[6, m], rows[7, m], rows[8, m] = a, t - ABOVE, c, 0
            for t in range(BELOW):
                m = (c * acqs + a) * BELOW + t
                rows[1, (c * acqs + a) * 16 + t] = m
                m += TOP
                rows[5, m], rows[6, m], rows[7, m], rows[8, m] = a, ROWS + t, c, 1
    rows[9, : QUANT * 8] = tap_table().reshape(-1)
    return rows


def kernel(
    acqs, peers, bands,
    shift_ref, fraction_ref, index_ref, image_ref, out_ref,
    offsets, x_ref, halo_out, halo_in, weight_ref, y_ref, z_ref,
    send, recv, lhs_ref, gram, column, back_send, back_recv,
    halo_send_sem, halo_recv_sem, send_sem, recv_sem, back_send_sem, back_recv_sem,
):
    f32, bf16 = jnp.float32, jnp.bfloat16
    me = lax.axis_index("acq")
    band = lax.axis_index("band")
    down = lax.rem(band + 1, bands)
    up = lax.rem(band + bands - 1, bands)

    barrier = pltpu.get_barrier_semaphore()

    def greet(k, carry):
        pl.semaphore_signal(
            barrier, inc=1, device_id={"acq": lax.rem(me + k, peers)}, device_id_type=MESH
        )
        return carry

    pl.semaphore_signal(barrier, inc=1, device_id={"band": down}, device_id_type=MESH)
    pl.semaphore_signal(barrier, inc=1, device_id={"band": up}, device_id_type=MESH)
    lax.fori_loop(1, peers, greet, 0)

    x_ref[...] = jnp.zeros_like(x_ref)
    for c in range(2):
        for a in range(acqs):
            at = (c * acqs + a) * 16
            x_ref[at : at + ROWS, : image_ref.shape[3]] = image_ref[c, a]
    x = x_ref[...]

    def chosen(row, count):
        wanted = lax.broadcasted_iota(jnp.int32, (count, LOCAL), 0).astype(f32)
        return (index_ref[row : row + 1, :LOCAL] == wanted).astype(f32).astype(bf16)

    halo_out[:TOP, :] = jnp.dot(chosen(0, TOP), x, preferred_element_type=f32).astype(bf16)
    halo_out[TOP:, :] = jnp.dot(chosen(1, BOTTOM), x, preferred_element_type=f32).astype(bf16)

    pl.semaphore_wait(barrier, peers + 1)
    to_down = pltpu.make_async_remote_copy(
        src_ref=halo_out.at[:TOP], dst_ref=halo_in.at[:TOP],
        send_sem=halo_send_sem.at[0], recv_sem=halo_recv_sem.at[0],
        device_id={"band": down}, device_id_type=MESH,
    )
    to_up = pltpu.make_async_remote_copy(
        src_ref=halo_out.at[TOP:], dst_ref=halo_in.at[TOP:],
        send_sem=halo_send_sem.at[1], recv_sem=halo_recv_sem.at[1],
        device_id={"band": up}, device_id_type=MESH,
    )
    to_down.start()
    to_up.start()

    offsets[...] = jnp.zeros_like(offsets)
    offsets[0, :acqs, :2] = shift_ref[...]
    offsets[1, :acqs, :2] = fraction_ref[...]
    lane = lax.broadcasted_iota(jnp.int32, (8, 128), 1)
    sub = lax.broadcasted_iota(jnp.int32, (8, 128), 0)

    def offset_weights(which):
        shift = offsets[0, :, which : which + 1]
        fraction = offsets[1, :, which : which + 1]
        taps = jnp.where((lane >> 3) == fraction, index_ref[9:10, :128], 0.0)
        for step in (8, 16, 32, 64):
            taps = taps + pltpu.roll(taps, step, 1)
        weights = []
        for off in range(1, 2 * HALO + 1):
            hit = (lane == off - (HALO - 3) - shift) & (lane < 8)
            weights.append(jnp.sum(jnp.where(hit, taps, 0.0), axis=1, keepdims=True))
        return weights

    row_weights = offset_weights(0)
    col_weights = offset_weights(1)

    sub_wide = lax.broadcasted_iota(jnp.int32, (8, 256), 0).astype(f32)
    no_top = jnp.where(band == 0, 0.0, -2.0).astype(f32)
    no_bottom = jnp.where(band == bands - 1, 1.0, -2.0).astype(f32)

    def row_matrix(at, halo):
        own = index_ref[at : at + 1, :] == sub_wide
        place = index_ref[at + 1 : at + 2, :]
        if halo:
            side = index_ref[8:9, :]
            own = own & (side != no_top) & (side != no_bottom)
        for r in range(ROWS):
            total = jnp.zeros((8, 256), f32)
            for off in range(1, 2 * HALO + 1):
                total = jnp.where(place == float(off - HALO + r), row_weights[off - 1], total)
            total = jnp.where(own, total, 0.0)
            for c in range(2):
                m = (c * ROWS + r) * 8
                weight_ref[m : m + 8, :] = jnp.where(
                    index_ref[at + 2 : at + 3, :] == float(c), total, 0.0
                )
        whole = weight_ref[...]
        high = whole.astype(bf16)
        low = (whole - high.astype(f32)).astype(bf16)
        return high, low

    high, low = row_matrix(2, False)
    y_ref[...] = jnp.dot(high[:, :LOCAL], x, preferred_element_type=f32) + jnp.dot(
        low[:, :LOCAL], x, preferred_element_type=f32
    )
    high, low = row_matrix(5, True)
    to_down.wait()
    to_up.wait()
    edge = halo_in[...]
    y_ref[...] += jnp.dot(high[:, :EDGE], edge, preferred_element_type=f32) + jnp.dot(
        low[:, :EDGE], edge, preferred_element_type=f32
    )

    for c in range(2):
        for r in range(ROWS):
            m = (c * ROWS + r) * 8
            y = y_ref[m : m + 8, :]
            z = jnp.zeros((8, LANES), f32)
            for off in range(1, 2 * HALO + 1):
                moved = y if off == HALO else pltpu.roll(y, (HALO - off) % LANES, 1)
                z = z + col_weights[off - 1] * moved
            z = jnp.concatenate([z, jnp.zeros((8, 256), f32)], axis=1)
            if r:
                z = pltpu.roll(z, BLOCK * r, 1)
            z_ref[m : m + 8, :] = z

    for j in range(peers):
        parts = []
        for c in range(2):
            pieces = [[], []]
            for r in range(ROWS):
                start = BLOCK * (j + r)
                end = start + BLOCK
                for v in range(start // 128, (end - 1) // 128 + 1):
                    pieces[v % 2].append((max(start - 128 * v, 0), r, v))
            halves = []
            for half in pieces:
                half.sort()
                value = None
                for begin, r, v in half:
                    m = (c * ROWS + r) * 8
                    piece = z_ref[m : m + 8, 128 * v : 128 * v + 128]
                    value = piece if value is None else jnp.where(lane >= begin, piece, value)
                halves.append(value)
            parts.append(jnp.concatenate(halves, axis=1))
        send[j] = jnp.concatenate(parts, axis=0).astype(bf16)

    recv[me] = send[me]

    def block_copy(src, dst):
        return pltpu.make_async_remote_copy(
            src_ref=send.at[dst], dst_ref=recv.at[src],
            send_sem=send_sem.at[dst], recv_sem=recv_sem.at[src],
            device_id={"acq": dst}, device_id_type=MESH,
        )

    def start_block(k, carry):
        block_copy(me, lax.rem(me + k, peers)).start()
        return carry

    def wait_block(k, carry):
        src = lax.rem(me + peers - k, peers)
        block_copy(src, src).wait_recv()
        return carry

    def wait_sent(k, carry):
        block_copy(me, lax.rem(me + k, peers)).wait_send()
        return carry

    lax.fori_loop(1, peers, start_block, 0)
    lax.fori_loop(1, peers, wait_block, 0)

    count = peers * 8
    blocks = recv[...].astype(f32)
    re = blocks[:, :8, :].reshape(count, RING)
    im = blocks[:, 8:, :].reshape(count, RING)
    wide = lax.broadcasted_iota(jnp.int32, (8, 2 * RING), 1)
    spot = lax.rem((wide & (RING - 1)) - BLOCK * me + 4 * RING, RING).astype(f32)
    in_row = spot - BLOCK * jnp.floor((spot + 0.5) * (1.0 / BLOCK))
    used = spot < BLOCK * ROWS
    first = jnp.where(used & (in_row < PATCH), 1.0, 0.0)[:1]
    second = jnp.where(used & (in_row >= PATCH), 1.0, 0.0)[:1]
    straight = jnp.concatenate([re, im], axis=1)
    crossed = jnp.concatenate([im, -re], axis=1)
    lhs_ref[0 * count : 1 * count] = (straight * first).astype(bf16)
    lhs_ref[1 * count : 2 * count] = (crossed * first).astype(bf16)
    lhs_ref[2 * count : 3 * count] = (straight * second).astype(bf16)
    lhs_ref[3 * count : 4 * count] = (crossed * second).astype(bf16)
    gram[...] = lax.dot_general(
        lhs_ref[...], straight.astype(bf16), (((1,), (1,)), ((), ())), preferred_element_type=f32
    )

    pixels = PATCH * PATCH
    groups = peers
    wide_lane = lax.broadcasted_iota(jnp.int32, (8, count), 1)
    wide_sub = lax.broadcasted_iota(jnp.int32, (8, count), 0)
    for p in range(2):
        cr = p * 2 * count
        ci = cr + count

        def diagonal(g, total):
            at = pl.multiple_of(g * 8, 8)
            mine = jnp.where(wide_lane == wide_sub + at, gram[pl.ds(cr + at, 8), :], 0.0)
            power = jnp.sum(mine, axis=1, keepdims=True) / pixels + 1e-06
            column[p, 0, pl.ds(at, 8), :] = jnp.broadcast_to(lax.rsqrt(power), (8, 128))
            return total + mine

        total = lax.fori_loop(0, groups, diagonal, jnp.zeros((8, count), f32), unroll=8)
        scale_row = lax.rsqrt(jnp.sum(total, axis=0, keepdims=True) / pixels + 1e-06)

        def by_columns(g, totals, first):
            tr, ti = totals
            at = pl.multiple_of(g * 8, 8)
            gr = gram[pl.ds(cr + at, 8), :]
            gi = gram[pl.ds(ci + at, 8), :]
            scale = column[p, 0, pl.ds(at, 8), :1]
            if first:
                return tr + gr * scale, ti - gi * scale
            ur = column[p, 1, pl.ds(at, 8), :1] * scale
            ui = column[p, 2, pl.ds(at, 8), :1] * scale
            return tr + (gr * ur + gi * ui), ti + (gr * ui - gi * ur)

        def by_rows(g, totals, ur, ui):
            at = pl.multiple_of(g * 8, 8)
            gr = gram[pl.ds(cr + at, 8), :]
            gi = gram[pl.ds(ci + at, 8), :]
            scale = column[p, 0, pl.ds(at, 8), :] * (1.0 / pixels)
            wr = jnp.sum(gr * ur - gi * ui, axis=1, keepdims=True) * scale
            wi = jnp.sum(gr * ui + gi * ur, axis=1, keepdims=True) * scale
            column[p, 1, pl.ds(at, 8), :] = wr
            column[p, 2, pl.ds(at, 8), :] = wi
            return totals + wr * wr + wi * wi

        def normalise(g, carry, inverse):
            at = pl.multiple_of(g * 8, 8)
            column[p, 1, pl.ds(at, 8), :] = column[p, 1, pl.ds(at, 8), :] * inverse
            column[p, 2, pl.ds(at, 8), :] = column[p, 2, pl.ds(at, 8), :] * inverse
            return carry

        norm = 2.0 * peers * acqs
        for step in range(0, ITERS, 2):
            zero = jnp.zeros((8, count), f32)
            tr, ti = lax.fori_loop(
                0, groups, functools.partial(by_columns, first=step == 0), (zero, zero), unroll=8
            )
            wr = jnp.sum(tr, axis=0, keepdims=True) * scale_row * (1.0 / pixels)
            wi = jnp.sum(ti, axis=0, keepdims=True) * scale_row * (1.0 / pixels)
            power = jnp.sum(wr * wr + wi * wi, axis=1, keepdims=True)
            inverse = lax.rsqrt(power / norm + 1e-06) * scale_row
            total = lax.fori_loop(
                0, groups,
                functools.partial(by_rows, ur=wr * inverse, ui=wi * inverse),
                jnp.zeros((8, 128), f32), unroll=8,
            )
            inverse = lax.rsqrt(jnp.sum(total, axis=0, keepdims=True) / norm + 1e-06)
            lax.fori_loop(0, groups, functools.partial(normalise, inverse=inverse), 0, unroll=8)

    def message(g, carry):
        at = pl.multiple_of(g * 8, 8)
        value = jnp.zeros((8, 128), f32)
        for p in range(2):
            for c in range(2):
                value = jnp.where((lane >> 3) == 2 * p + c, column[p, 1 + c, pl.ds(at, 8), :], value)
        value = jnp.where((lane & 7) == sub, value, 0.0)
        back_send[g] = jnp.sum(value, axis=0, keepdims=True)
        return carry

    lax.fori_loop(0, groups, message, 0, unroll=8)
    back_recv[me] = back_send[me]

    def back_copy(src, dst):
        return pltpu.make_async_remote_copy(
            src_ref=back_send.at[dst], dst_ref=back_recv.at[src],
            send_sem=back_send_sem.at[dst], recv_sem=back_recv_sem.at[src],
            device_id={"acq": dst}, device_id_type=MESH,
        )

    def start_back(k, carry):
        back_copy(me, lax.rem(me + k, peers)).start()
        return carry

    def wait_back(k, carry):
        src = lax.rem(me + peers - k, peers)
        back_copy(src, src).wait_recv()
        return carry

    def wait_back_sent(k, carry):
        back_copy(me, lax.rem(me + k, peers)).wait_send()
        return carry

    lax.fori_loop(1, peers, start_back, 0)
    lax.fori_loop(1, peers, wait_sent, 0)
    lax.fori_loop(1, peers, wait_back, 0)

    values = back_recv[...].reshape(peers, 128)
    into = lax.broadcasted_iota(jnp.int32, (peers, 2 * peers), 1)
    source = lax.broadcasted_iota(jnp.int32, (peers, 2 * peers), 0)
    result = jnp.zeros((16, 2 * peers), f32)
    for p in range(2):
        result = result + lax.dot_general(
            values[:, 16 * p : 16 * p + 16], (into == 2 * source + p).astype(f32),
            (((0,), (0,)), ((), ())), precision=lax.Precision.HIGHEST, preferred_element_type=f32,
        )
    for c in range(2):
        out_ref[c, :, 0, :] = result[8 * c : 8 * c + acqs]
    lax.fori_loop(1, peers, wait_back_sent, 0)


def on_device(images, pixel_shift, fraction_index):
    acqs = images.shape[1]
    peers = lax.axis_size("acq")
    bands = lax.axis_size("band")
    f32, bf16 = jnp.float32, jnp.bfloat16
    vmem = pl.BlockSpec(memory_space=pltpu.VMEM)
    dma = pltpu.SemaphoreType.DMA
    return pl.pallas_call(
        functools.partial(kernel, acqs, peers, bands),
        out_shape=jax.ShapeDtypeStruct((2, acqs, 1, 2 * peers), f32),
        in_specs=[vmem] * 4,
        out_specs=vmem,
        scratch_shapes=[
            pltpu.VMEM((2, 8, 128), jnp.int32),
            pltpu.VMEM((LOCAL, LANES), bf16),
            pltpu.VMEM((EDGE, LANES), bf16),
            pltpu.VMEM((EDGE, LANES), bf16),
            pltpu.VMEM((2 * ROWS * 8, 256), f32),
            pltpu.VMEM((2 * ROWS * 8, LANES), f32),
            pltpu.VMEM((2 * ROWS * 8, LANES + 256), f32),
            pltpu.VMEM((peers, 16, RING), bf16),
            pltpu.VMEM((peers, 16, RING), bf16),
            pltpu.VMEM((4 * peers * 8, 2 * RING), bf16),
            pltpu.VMEM((4 * peers * 8, peers * 8), f32),
            pltpu.VMEM((2, 3, peers * 8, 128), f32),
            pltpu.VMEM((peers, 1, 128), f32),
            pltpu.VMEM((peers, 1, 128), f32),
            dma((2,)), dma((2,)),
            dma((peers,)), dma((peers,)),
            dma((peers,)), dma((peers,)),
        ],
        compiler_params=pltpu.CompilerParams(
            collective_id=0, has_side_effects=True, vmem_limit_bytes=48 * 1024 * 1024
        ),
    )(pixel_shift, fraction_index, jnp.asarray(index_rows(acqs)), images)


def solution(mesh):
    placed = (P(None, "acq", "band", None), P("acq", None), P("acq", None))
    return jax.shard_map(
        on_device,
        mesh=mesh,
        in_specs=placed,
        out_specs=P(None, "acq", "band", None),
        check_vma=False,
    )
```

```python
import functools

import jax
import jax.numpy as jnp
import numpy as np
from jax import lax
from jax.experimental import pallas as pl
from jax.experimental.pallas import tpu as pltpu
from jax.sharding import PartitionSpec as P

PATCH = 11
QUANT = 16
HALO = 7
ITERS = 4
MESH = pl.DeviceIdType.MESH

ROWS = 11
LANES = 768
BLOCK = 22
RING = 256
ABOVE = 6
BELOW = 7
TOP = 80
BOTTOM = 96
LOCAL = 192
EDGE = TOP + BOTTOM


def tap_table():
    fraction = np.arange(QUANT, dtype=np.float64)[:, None] / QUANT
    where_at = np.arange(8, dtype=np.float64)[None, :] - 3.0 - fraction
    raw_taps = np.sinc(where_at) * (0.5 + 0.5 * np.cos(np.pi * where_at / 4.0))
    return (raw_taps / raw_taps.sum(axis=1, keepdims=True)).astype(np.float32)


def index_rows(acqs):
    rows = np.full((16, 256), -1, np.float32)
    for c in range(2):
        for a in range(acqs):
            for i in range(ROWS):
                k = (c * acqs + a) * 16 + i
                rows[2, k], rows[3, k], rows[4, k] = a, i, c
            for t in range(ABOVE):
                m = (c * acqs + a) * ABOVE + t
                rows[0, (c * acqs + a) * 16 + ROWS - ABOVE + t] = m
                rows[5, m], rows[6, m], rows[7, m], rows[8, m] = a, t - ABOVE, c, 0
            for t in range(BELOW):
                m = (c * acqs + a) * BELOW + t
                rows[1, (c * acqs + a) * 16 + t] = m
                m += TOP
                rows[5, m], rows[6, m], rows[7, m], rows[8, m] = a, ROWS + t, c, 1
    rows[9, : QUANT * 8] = tap_table().reshape(-1)
    return rows


def kernel(
    acqs, peers, bands,
    shift_hbm, fraction_hbm, index_hbm, image_hbm, out_ref,
    shift_ref, fraction_ref, index_ref, image_ref, offsets, x_ref, halo_out, halo_in, weight_ref, y_ref, z_ref,
    send, recv, lhs_ref, gram, column, back_send, back_recv,
    fetch_sem, join_sem, go_sem,
    halo_send_sem, halo_recv_sem, send_sem, recv_sem, back_send_sem, back_recv_sem,
):
    f32, bf16 = jnp.float32, jnp.bfloat16
    me = lax.axis_index("acq")
    band = lax.axis_index("band")
    down = lax.rem(band + 1, bands)
    up = lax.rem(band + bands - 1, bands)

    barrier = pltpu.get_barrier_semaphore()

    root = min(1, peers - 1)

    def greet(k, carry):
        pl.semaphore_signal(
            barrier, inc=1, device_id={"acq": lax.rem(me + k, peers)}, device_id_type=MESH
        )
        return carry

    def let_go(k, carry):
        pl.semaphore_signal(
            go_sem, inc=1, device_id={"acq": lax.rem(me + k, peers)}, device_id_type=MESH
        )
        return carry

    pl.semaphore_signal(barrier, inc=1, device_id={"band": down}, device_id_type=MESH)
    pl.semaphore_signal(barrier, inc=1, device_id={"band": up}, device_id_type=MESH)

    @pl.when(me == root)
    def _():
        lax.fori_loop(1, peers, greet, 0)

    fetches = [
        pltpu.make_async_copy(src, dst, fetch_sem.at[i])
        for i, (src, dst) in enumerate(
            ((image_hbm, image_ref), (index_hbm, index_ref), (shift_hbm, shift_ref),
             (fraction_hbm, fraction_ref))
        )
    ]
    for fetch in fetches:
        fetch.start()

    x_ref[...] = jnp.zeros_like(x_ref)
    for fetch in fetches:
        fetch.wait()
    for c in range(2):
        for a in range(acqs):
            at = (c * acqs + a) * 16
            x_ref[at : at + ROWS, : image_ref.shape[3]] = image_ref[c, a]
    x = x_ref[...]

    def chosen(row, count):
        wanted = lax.broadcasted_iota(jnp.int32, (count, LOCAL), 0).astype(f32)
        return (index_ref[row : row + 1, :LOCAL] == wanted).astype(f32).astype(bf16)

    halo_out[:TOP, :] = jnp.dot(chosen(0, TOP), x, preferred_element_type=f32).astype(bf16)
    halo_out[TOP:, :] = jnp.dot(chosen(1, BOTTOM), x, preferred_element_type=f32).astype(bf16)

    @pl.when(me == root)
    def _():
        pl.semaphore_wait(barrier, 2)

    @pl.when(me != root)
    def _():
        pl.semaphore_wait(barrier, 3)
        pl.semaphore_signal(join_sem, inc=1, device_id={"acq": root}, device_id_type=MESH)

    to_down = pltpu.make_async_remote_copy(
        src_ref=halo_out.at[:TOP], dst_ref=halo_in.at[:TOP],
        send_sem=halo_send_sem.at[0], recv_sem=halo_recv_sem.at[0],
        device_id={"band": down}, device_id_type=MESH,
    )
    to_up = pltpu.make_async_remote_copy(
        src_ref=halo_out.at[TOP:], dst_ref=halo_in.at[TOP:],
        send_sem=halo_send_sem.at[1], recv_sem=halo_recv_sem.at[1],
        device_id={"band": up}, device_id_type=MESH,
    )
    to_down.start()
    to_up.start()

    offsets[...] = jnp.zeros_like(offsets)
    offsets[0, :acqs, :2] = shift_ref[...]
    offsets[1, :acqs, :2] = fraction_ref[...]
    lane = lax.broadcasted_iota(jnp.int32, (8, 128), 1)
    sub = lax.broadcasted_iota(jnp.int32, (8, 128), 0)

    def offset_weights(which):
        shift = offsets[0, :, which : which + 1]
        fraction = offsets[1, :, which : which + 1]
        taps = jnp.where((lane >> 3) == fraction, index_ref[9:10, :128], 0.0)
        for step in (8, 16, 32, 64):
            taps = taps + pltpu.roll(taps, step, 1)
        weights = []
        for off in range(1, 2 * HALO + 1):
            hit = (lane == off - (HALO - 3) - shift) & (lane < 8)
            weights.append(jnp.sum(jnp.where(hit, taps, 0.0), axis=1, keepdims=True))
        return weights

    row_weights = offset_weights(0)
    col_weights = offset_weights(1)

    sub_wide = lax.broadcasted_iota(jnp.int32, (8, 256), 0).astype(f32)
    no_top = jnp.where(band == 0, 0.0, -2.0).astype(f32)
    no_bottom = jnp.where(band == bands - 1, 1.0, -2.0).astype(f32)

    def row_matrix(at, halo):
        own = index_ref[at : at + 1, :] == sub_wide
        place = index_ref[at + 1 : at + 2, :]
        if halo:
            side = index_ref[8:9, :]
            own = own & (side != no_top) & (side != no_bottom)
        for r in range(ROWS):
            total = jnp.zeros((8, 256), f32)
            for off in range(1, 2 * HALO + 1):
                total = jnp.where(place == float(off - HALO + r), row_weights[off - 1], total)
            total = jnp.where(own, total, 0.0)
            for c in range(2):
                m = (c * ROWS + r) * 8
                weight_ref[m : m + 8, :] = jnp.where(
                    index_ref[at + 2 : at + 3, :] == float(c), total, 0.0
                )
        whole = weight_ref[...]
        high = whole.astype(bf16)
        low = (whole - high.astype(f32)).astype(bf16)
        return high, low

    high, low = row_matrix(2, False)
    y_ref[...] = jnp.dot(high[:, :LOCAL], x, preferred_element_type=f32) + jnp.dot(
        low[:, :LOCAL], x, preferred_element_type=f32
    )
    high, low = row_matrix(5, True)
    to_down.wait()
    to_up.wait()
    edge = halo_in[...]
    y_ref[...] += jnp.dot(high[:, :EDGE], edge, preferred_element_type=f32) + jnp.dot(
        low[:, :EDGE], edge, preferred_element_type=f32
    )

    for c in range(2):
        for r in range(ROWS):
            m = (c * ROWS + r) * 8
            y = y_ref[m : m + 8, :]
            z = jnp.zeros((8, LANES), f32)
            for off in range(1, 2 * HALO + 1):
                moved = y if off == HALO else pltpu.roll(y, (HALO - off) % LANES, 1)
                z = z + col_weights[off - 1] * moved
            z = jnp.concatenate([z, jnp.zeros((8, 256), f32)], axis=1)
            if r:
                z = pltpu.roll(z, BLOCK * r, 1)
            z_ref[m : m + 8, :] = z

    for j in range(peers):
        parts = []
        for c in range(2):
            pieces = [[], []]
            for r in range(ROWS):
                start = BLOCK * (j + r)
                end = start + BLOCK
                for v in range(start // 128, (end - 1) // 128 + 1):
                    pieces[v % 2].append((max(start - 128 * v, 0), r, v))
            halves = []
            for half in pieces:
                half.sort()
                value = None
                for begin, r, v in half:
                    m = (c * ROWS + r) * 8
                    piece = z_ref[m : m + 8, 128 * v : 128 * v + 128]
                    value = piece if value is None else jnp.where(lane >= begin, piece, value)
                halves.append(value)
            parts.append(jnp.concatenate(halves, axis=1))
        send[j] = jnp.concatenate(parts, axis=0).astype(bf16)

    recv[me] = send[me]

    def block_copy(src, dst):
        return pltpu.make_async_remote_copy(
            src_ref=send.at[dst], dst_ref=recv.at[src],
            send_sem=send_sem.at[dst], recv_sem=recv_sem.at[src],
            device_id={"acq": dst}, device_id_type=MESH,
        )

    def start_block(k, carry):
        block_copy(me, lax.rem(me + k, peers)).start()
        return carry

    def wait_block(k, carry):
        src = lax.rem(me + peers - k, peers)
        block_copy(src, src).wait_recv()
        return carry

    def wait_sent(k, carry):
        block_copy(me, lax.rem(me + k, peers)).wait_send()
        return carry

    @pl.when(me == root)
    def _():
        pl.semaphore_wait(join_sem, peers - 1)
        lax.fori_loop(1, peers, let_go, 0)

    @pl.when(me != root)
    def _():
        pl.semaphore_wait(go_sem, 1)

    lax.fori_loop(1, peers, start_block, 0)
    lax.fori_loop(1, peers, wait_block, 0)

    count = peers * 8
    blocks = recv[...].astype(f32)
    re = blocks[:, :8, :].reshape(count, RING)
    im = blocks[:, 8:, :].reshape(count, RING)
    wide = lax.broadcasted_iota(jnp.int32, (8, 2 * RING), 1)
    spot = lax.rem((wide & (RING - 1)) - BLOCK * me + 4 * RING, RING).astype(f32)
    in_row = spot - BLOCK * jnp.floor((spot + 0.5) * (1.0 / BLOCK))
    used = spot < BLOCK * ROWS
    first = jnp.where(used & (in_row < PATCH), 1.0, 0.0)[:1]
    second = jnp.where(used & (in_row >= PATCH), 1.0, 0.0)[:1]
    straight = jnp.concatenate([re, im], axis=1)
    crossed = jnp.concatenate([im, -re], axis=1)
    lhs_ref[0 * count : 1 * count] = (straight * first).astype(bf16)
    lhs_ref[1 * count : 2 * count] = (crossed * first).astype(bf16)
    lhs_ref[2 * count : 3 * count] = (straight * second).astype(bf16)
    lhs_ref[3 * count : 4 * count] = (crossed * second).astype(bf16)
    gram[...] = lax.dot_general(
        lhs_ref[...], straight.astype(bf16), (((1,), (1,)), ((), ())), preferred_element_type=f32
    )

    groups = peers
    norm = 2.0 * peers * acqs
    both = (0, 1)

    def load(p, part, at):
        return gram[pl.ds((2 * p + part) * count + at, 8), :]

    def twice(value):
        return jnp.concatenate([value] * (count // 128), axis=1)

    def diagonal(g, totals, half):
        at = pl.multiple_of(g * 8, 8)
        new = []
        for p in both:
            mine = jnp.where(
                lane == sub + (at - 128 * half), load(p, 0, at)[:, 128 * half : 128 * half + 128], 0.0
            )
            power = jnp.sum(mine, axis=1, keepdims=True) / (PATCH * PATCH) + 1e-06
            column[p, 0, pl.ds(at, 8), :] = jnp.broadcast_to(lax.rsqrt(power) / PATCH, (8, 128))
            new.append(totals[p] + mine)
        return tuple(new)

    scale_rows = [[], []]
    for half in range(count // 128):
        totals = lax.fori_loop(
            16 * half, 16 * half + 16, functools.partial(diagonal, half=half),
            (jnp.zeros((8, 128), f32),) * 2, unroll=8,
        )
        for p in both:
            power = jnp.sum(totals[p], axis=0, keepdims=True) / (PATCH * PATCH) + 1e-06
            scale_rows[p].append(lax.rsqrt(power) / PATCH)
    scale_rows = [jnp.concatenate(rows, axis=1) for rows in scale_rows]

    def by_columns(g, totals, first):
        at = pl.multiple_of(g * 8, 8)
        new = []
        for p in both:
            tr, ti = totals[p]
            gr, gi = load(p, 0, at), load(p, 1, at)
            if first:
                scale = twice(column[p, 0, pl.ds(at, 8), :])
                new.append((tr + gr * scale, ti - gi * scale))
            else:
                ur = twice(column[p, 1, pl.ds(at, 8), :])
                ui = twice(column[p, 2, pl.ds(at, 8), :])
                new.append((tr + (gr * ur + gi * ui), ti + (gr * ui - gi * ur)))
        return tuple(new)

    def by_rows(g, totals, vectors, last):
        at = pl.multiple_of(g * 8, 8)
        new = []
        for p in both:
            ur, ui = vectors[p]
            gr, gi = load(p, 0, at), load(p, 1, at)
            scale = column[p, 0, pl.ds(at, 8), :]
            wr = jnp.sum(gr * ur - gi * ui, axis=1, keepdims=True) * scale
            wi = jnp.sum(gr * ui + gi * ur, axis=1, keepdims=True) * scale
            column[p, 1, pl.ds(at, 8), :] = wr if last else wr * scale
            column[p, 2, pl.ds(at, 8), :] = wi if last else wi * scale
            new.append(totals[p] + (wr * wr + wi * wi))
        return tuple(new)

    inverses = [None, None]
    for step in range(0, ITERS, 2):
        zero = jnp.zeros((8, count), f32)
        totals = lax.fori_loop(
            0, groups, functools.partial(by_columns, first=step == 0), ((zero, zero),) * 2, unroll=16
        )
        vectors = []
        for p in both:
            scale = scale_rows[p] if step == 0 else scale_rows[p] * inverses[p][:, :1]
            wr = jnp.sum(totals[p][0], axis=0, keepdims=True) * scale
            wi = jnp.sum(totals[p][1], axis=0, keepdims=True) * scale
            power = jnp.sum(wr * wr + wi * wi, axis=1, keepdims=True)
            scale = lax.rsqrt(power / norm + 1e-06) * scale_rows[p]
            vectors.append(tuple(jnp.broadcast_to(w * scale, (8, count)) for w in (wr, wi)))
        totals = lax.fori_loop(
            0, groups, functools.partial(by_rows, vectors=vectors, last=step + 2 == ITERS),
            (jnp.zeros((8, 128), f32),) * 2, unroll=16,
        )
        for p in both:
            power = jnp.sum(totals[p], axis=0, keepdims=True)
            inverses[p] = lax.rsqrt(power / norm + 1e-06)

    choice = lane >> 3
    factor = jnp.where((lane & 7) == sub, jnp.where(choice < 2, inverses[0], inverses[1]), 0.0)
    factor = jnp.where(choice < 4, factor, 0.0)

    def message(g, carry):
        at = pl.multiple_of(g * 8, 8)
        re = jnp.where(choice < 2, column[0, 1, pl.ds(at, 8), :], column[1, 1, pl.ds(at, 8), :])
        im = jnp.where(choice < 2, column[0, 2, pl.ds(at, 8), :], column[1, 2, pl.ds(at, 8), :])
        value = jnp.where((choice & 1) == 0, re, im) * factor
        back_send[g] = jnp.sum(value, axis=0, keepdims=True)
        return carry

    lax.fori_loop(0, groups, message, 0, unroll=16)
    back_recv[me] = back_send[me]

    def back_copy(src, dst):
        return pltpu.make_async_remote_copy(
            src_ref=back_send.at[dst], dst_ref=back_recv.at[src],
            send_sem=back_send_sem.at[dst], recv_sem=back_recv_sem.at[src],
            device_id={"acq": dst}, device_id_type=MESH,
        )

    def start_back(k, carry):
        back_copy(me, lax.rem(me + k, peers)).start()
        return carry

    def wait_back(k, carry):
        src = lax.rem(me + peers - k, peers)
        back_copy(src, src).wait_recv()
        return carry

    def wait_back_sent(k, carry):
        back_copy(me, lax.rem(me + k, peers)).wait_send()
        return carry

    lax.fori_loop(1, peers, start_back, 0)
    lax.fori_loop(1, peers, wait_sent, 0)
    lax.fori_loop(1, peers, wait_back, 0)

    values = back_recv[...].reshape(peers, 128)
    into = lax.broadcasted_iota(jnp.int32, (peers, 2 * peers), 1)
    source = lax.broadcasted_iota(jnp.int32, (peers, 2 * peers), 0)
    result = jnp.zeros((16, 2 * peers), f32)
    for p in range(2):
        result = result + lax.dot_general(
            values[:, 16 * p : 16 * p + 16], (into == 2 * source + p).astype(f32),
            (((0,), (0,)), ((), ())), precision=lax.Precision.HIGHEST, preferred_element_type=f32,
        )
    for c in range(2):
        out_ref[c, :, 0, :] = result[8 * c : 8 * c + acqs]
    lax.fori_loop(1, peers, wait_back_sent, 0)


def on_device(images, pixel_shift, fraction_index):
    acqs = images.shape[1]
    peers = lax.axis_size("acq")
    bands = lax.axis_size("band")
    f32, bf16 = jnp.float32, jnp.bfloat16
    vmem = pl.BlockSpec(memory_space=pltpu.VMEM)
    dma = pltpu.SemaphoreType.DMA
    return pl.pallas_call(
        functools.partial(kernel, acqs, peers, bands),
        out_shape=jax.ShapeDtypeStruct((2, acqs, 1, 2 * peers), f32),
        in_specs=[pl.BlockSpec(memory_space=pltpu.HBM)] * 4,
        out_specs=vmem,
        scratch_shapes=[
            pltpu.VMEM(pixel_shift.shape, jnp.int32),
            pltpu.VMEM(fraction_index.shape, jnp.int32),
            pltpu.VMEM((16, 256), f32),
            pltpu.VMEM(images.shape, bf16),
            pltpu.VMEM((2, 8, 128), jnp.int32),
            pltpu.VMEM((LOCAL, LANES), bf16),
            pltpu.VMEM((EDGE, LANES), bf16),
            pltpu.VMEM((EDGE, LANES), bf16),
            pltpu.VMEM((2 * ROWS * 8, 256), f32),
            pltpu.VMEM((2 * ROWS * 8, LANES), f32),
            pltpu.VMEM((2 * ROWS * 8, LANES + 256), f32),
            pltpu.VMEM((peers, 16, RING), bf16),
            pltpu.VMEM((peers, 16, RING), bf16),
            pltpu.VMEM((4 * peers * 8, 2 * RING), bf16),
            pltpu.VMEM((4 * peers * 8, peers * 8), f32),
            pltpu.VMEM((2, 3, peers * 8, 128), f32),
            pltpu.VMEM((peers, 1, 128), f32),
            pltpu.VMEM((peers, 1, 128), f32),
            dma((4,)), pltpu.SemaphoreType.REGULAR, pltpu.SemaphoreType.REGULAR,
            dma((2,)), dma((2,)),
            dma((peers,)), dma((peers,)),
            dma((peers,)), dma((peers,)),
        ],
        compiler_params=pltpu.CompilerParams(
            collective_id=0, has_side_effects=True, vmem_limit_bytes=48 * 1024 * 1024
        ),
    )(pixel_shift, fraction_index, jnp.asarray(index_rows(acqs)), images)


def solution(mesh):
    placed = (P(None, "acq", "band", None), P("acq", None), P("acq", None))
    return jax.shard_map(
        on_device,
        mesh=mesh,
        in_specs=placed,
        out_specs=P(None, "acq", "band", None),
        check_vma=False,
    )
```

```python
import functools

import jax
import jax.numpy as jnp
import numpy as np
from jax import lax
from jax.experimental import pallas as pl
from jax.experimental.pallas import tpu as pltpu
from jax.sharding import PartitionSpec as P

PATCH = 11
QUANT = 16
HALO = 7
ITERS = 4
MESH = pl.DeviceIdType.MESH

ROWS = 11
LANES = 768
BLOCK = 22
RING = 256
ABOVE = 6
BELOW = 7
TOP = 72
BOTTOM = 88
LOCAL = 192
EDGE = TOP + BOTTOM


def tap_table():
    fraction = np.arange(QUANT, dtype=np.float64)[:, None] / QUANT
    where_at = np.arange(8, dtype=np.float64)[None, :] - 3.0 - fraction
    raw_taps = np.sinc(where_at) * (0.5 + 0.5 * np.cos(np.pi * where_at / 4.0))
    return (raw_taps / raw_taps.sum(axis=1, keepdims=True)).astype(np.float32)


def index_rows(acqs):
    rows = np.full((16, 256), -1, np.float32)
    for c in range(2):
        for a in range(acqs):
            for i in range(ROWS):
                k = (c * acqs + a) * 16 + i
                rows[2, k], rows[3, k], rows[4, k] = a, i, c
            for t in range(ABOVE):
                m = (c * acqs + a) * ABOVE + t
                rows[0, (c * acqs + a) * 16 + ROWS - ABOVE + t] = m
                rows[5, m], rows[6, m], rows[7, m] = a, t - ABOVE, c
            for t in range(BELOW):
                m = (c * acqs + a) * BELOW + t
                rows[1, (c * acqs + a) * 16 + t] = m
                m += TOP
                rows[5, m], rows[6, m], rows[7, m] = a, ROWS + t, c
    rows[8, : QUANT * 8] = tap_table().reshape(-1)
    return rows


def kernel(
    acqs, peers, bands,
    shift_ref, fraction_ref, index_ref, image_ref, out_ref,
    offsets, x_ref, halo_out, halo_in, weight_ref, y_ref, z_ref, moved_ref,
    send, recv, lhs_ref, gram, column, back_send, back_recv,
    join_sem, go_sem,
    halo_send_sem, halo_recv_sem, send_sem, recv_sem, back_send_sem, back_recv_sem,
):
    f32, bf16 = jnp.float32, jnp.bfloat16
    me = lax.axis_index("acq")
    band = lax.axis_index("band")
    has_up, has_down = band > 0, band < bands - 1
    down = lax.min(band + 1, bands - 1)
    up = lax.max(band - 1, 0)

    barrier = pltpu.get_barrier_semaphore()

    root = min(1, peers - 1)

    def greet(k, carry):
        pl.semaphore_signal(
            barrier, inc=1, device_id={"acq": lax.rem(me + k, peers)}, device_id_type=MESH
        )
        return carry

    def let_go(k, carry):
        pl.semaphore_signal(
            go_sem, inc=1, device_id={"acq": lax.rem(me + k, peers)}, device_id_type=MESH
        )
        return carry

    @pl.when(has_down)
    def _():
        pl.semaphore_signal(barrier, inc=1, device_id={"band": down}, device_id_type=MESH)

    @pl.when(has_up)
    def _():
        pl.semaphore_signal(barrier, inc=1, device_id={"band": up}, device_id_type=MESH)

    @pl.when(me == root)
    def _():
        lax.fori_loop(1, peers, greet, 0)

    x_ref[...] = jnp.zeros_like(x_ref)
    for c in range(2):
        for a in range(acqs):
            at = (c * acqs + a) * 16
            x_ref[at : at + ROWS, : image_ref.shape[3]] = image_ref[c, a]
    x = x_ref[...]

    def chosen(row, count):
        wanted = lax.broadcasted_iota(jnp.int32, (count, LOCAL), 0).astype(f32)
        return (index_ref[row : row + 1, :LOCAL] == wanted).astype(f32).astype(bf16)

    cols = image_ref.shape[3]
    for row, at, count in ((0, 0, TOP), (1, TOP, BOTTOM)):
        rows = jnp.dot(chosen(row, count), x, preferred_element_type=f32)[:, :cols]
        halo_out[at // 8 : (at + count) // 8] = rows.reshape(count // 8, 8, cols).astype(bf16)

    greeters = (
        has_up.astype(jnp.int32) + has_down.astype(jnp.int32) + (me != root).astype(jnp.int32)
    )
    pl.semaphore_wait(barrier, greeters)

    @pl.when(me != root)
    def _():
        pl.semaphore_signal(join_sem, inc=1, device_id={"acq": root}, device_id_type=MESH)

    to_down = pltpu.make_async_remote_copy(
        src_ref=halo_out.at[: TOP // 8], dst_ref=halo_in.at[: TOP // 8],
        send_sem=halo_send_sem.at[0], recv_sem=halo_recv_sem.at[0],
        device_id={"band": down}, device_id_type=MESH,
    )
    to_up = pltpu.make_async_remote_copy(
        src_ref=halo_out.at[TOP // 8 :], dst_ref=halo_in.at[TOP // 8 :],
        send_sem=halo_send_sem.at[1], recv_sem=halo_recv_sem.at[1],
        device_id={"band": up}, device_id_type=MESH,
    )

    @pl.when(has_down)
    def _():
        to_down.start()

    @pl.when(has_up)
    def _():
        to_up.start()

    @pl.when(jnp.logical_not(has_up))
    def _():
        halo_in[: TOP // 8] = jnp.zeros((TOP // 8, 8, cols), bf16)

    @pl.when(jnp.logical_not(has_down))
    def _():
        halo_in[TOP // 8 :] = jnp.zeros((BOTTOM // 8, 8, cols), bf16)

    offsets[...] = jnp.zeros_like(offsets)
    offsets[0, :2, :acqs] = shift_ref[...]
    offsets[1, :2, :acqs] = fraction_ref[...]
    lane = lax.broadcasted_iota(jnp.int32, (8, 128), 1)
    sub = lax.broadcasted_iota(jnp.int32, (8, 128), 0)

    held = (jnp.where(sub < acqs, sub, sub - 2), sub & 3)
    held_part = (jnp.where(sub < acqs, 0.0, 1.0), jnp.ones((8, 128), f32))

    def offset_weights(which, group):
        shift, fraction = (
            jnp.sum(
                jnp.where(lane == held[group], offsets[i, which : which + 1, :], 0),
                axis=1, keepdims=True,
            )
            for i in range(2)
        )
        taps = jnp.where((lane >> 3) == fraction, index_ref[8:9, :128], 0.0)
        for step in (8, 16, 32, 64):
            taps = taps + pltpu.roll(taps, step, 1)
        weights = []
        for off in range(1, 2 * HALO + 1):
            hit = (lane == off - (HALO - 3) - shift) & (lane < 8)
            weights.append(jnp.sum(jnp.where(hit, taps, 0.0), axis=1, keepdims=True))
        return weights

    row_weights = [offset_weights(0, group) for group in range(2)]
    col_weights = [offset_weights(1, group) for group in range(2)]

    def row_matrix(at):
        place = index_ref[at + 1 : at + 2, :]
        own = []
        for group in range(2):
            acq = jnp.concatenate([held[group].astype(f32)] * 2, axis=1)
            part = jnp.concatenate([held_part[group]] * 2, axis=1)
            own.append((index_ref[at : at + 1, :] == acq) & (index_ref[at + 2 : at + 3, :] == part))
        for r in range(ROWS):
            totals = [jnp.zeros((8, 256), f32)] * 2
            for off in range(1, 2 * HALO + 1):
                hit = place == float(off - HALO + r)
                for group in range(2):
                    totals[group] = jnp.where(hit, row_weights[group][off - 1], totals[group])
            for group in range(2):
                m = (r * 2 + group) * 8
                weight_ref[m : m + 8, :] = jnp.where(own[group], totals[group], 0.0)
        whole = weight_ref[...]
        high = whole.astype(bf16)
        low = (whole - high.astype(f32)).astype(bf16)
        return high, low

    high, low = row_matrix(2)
    y_ref[...] = jnp.dot(high[:, :LOCAL], x, preferred_element_type=f32) + jnp.dot(
        low[:, :LOCAL], x, preferred_element_type=f32
    )
    high, low = row_matrix(5)

    @pl.when(has_up)
    def _():
        to_down.wait_recv()

    @pl.when(has_down)
    def _():
        to_up.wait_recv()
    edge = halo_in[...].reshape(EDGE, cols)
    y_ref[:, :cols] += jnp.dot(high[:, :EDGE], edge, preferred_element_type=f32) + jnp.dot(
        low[:, :EDGE], edge, preferred_element_type=f32
    )

    for r in range(ROWS):
        parts = []
        for group in range(2):
            m = (r * 2 + group) * 8
            y = y_ref[m : m + 8, :]
            moved = [y] + [pltpu.roll(y, LANES - low, 1) for low in range(1, 4)]
            z = None
            for high in range(4):
                total = None
                for low in range(4):
                    off = 4 * high + low
                    if 1 <= off <= 2 * HALO:
                        term = col_weights[group][off - 1] * moved[low]
                        total = term if total is None else total + term
                if 4 * high != 8:
                    total = pltpu.roll(total, (8 - 4 * high) % LANES, 1)
                z = total if z is None else z + total
            z = jnp.concatenate([z, jnp.zeros((8, 256), f32)], axis=1)
            parts.append(pltpu.roll(z, (BLOCK * r + LANES + 256 - 1) % (LANES + 256), 1))
        z_ref[r] = jnp.concatenate(parts, axis=0).astype(bf16)

    def bits(v):
        place = lax.broadcasted_iota(jnp.int32, (16, 128), 1).astype(f32) + (128.0 * v + 0.5)
        rest = jnp.floor(place * (1.0 / BLOCK))
        rest = rest - 16.0 * jnp.floor(rest * (1.0 / 16))
        found = []
        for bit in (8.0, 4.0, 2.0, 1.0):
            hit = jnp.where(rest >= bit, 1.0, 0.0)
            rest = rest - bit * hit
            found.append(hit.astype(bf16) > 0.5)
        return found[::-1]

    for v in range((LANES + 256) // 128):
        rows = [z_ref[r, :, 128 * v : 128 * v + 128] for r in range(ROWS)]
        rows = rows + rows[: 16 - ROWS]
        for k, hit in enumerate(bits(v)):
            rows = [jnp.where(hit, rows[(i + (1 << k)) % 16], rows[i]) for i in range(16)]
        for i in range(16):
            moved_ref[v, i] = rows[i]

    narrow = lax.broadcasted_iota(jnp.int32, (16, 128), 1).astype(f32).astype(bf16)
    upper = lax.broadcasted_iota(jnp.int32, (16, 128), 0).astype(f32).astype(bf16) < 12.0
    for j in range(peers):
        start = BLOCK * j
        halves = []
        for half in range(2):
            used = [
                v for v in range(start // 128, (start + BLOCK * ROWS - 1) // 128 + 1) if v % 2 == half
            ]
            value = moved_ref[used[-1], -j % 16]
            if len(used) == 2:
                value = jnp.where(
                    narrow >= float(start - 128 * used[0]), moved_ref[used[0], -j % 16], value
                )
            halves.append(value)
        send[j, 0:8, :] = halves[0][:8]
        send[j, 8:16, :] = halves[1][:8]
        send[j, 16:24, :] = jnp.where(upper, halves[0], halves[1])[8:]

    recv[me] = send[me]

    ys = [lax.rem(me // 8 + d, 4) * 8 for d in range(4)]
    xs = [lax.rem(lax.rem(me // 2, 4) + d, 4) * 2 for d in range(4)]
    cores = [lax.rem(me, 2), 1 - lax.rem(me, 2)]
    moves = sorted(
        ((dy, dx, dc) for dy in range(4) for dx in range(4) for dc in range(2) if dy or dx or dc),
        key=lambda move: -(4 * min(move[0], 4 - move[0]) + 2 * min(move[1], 4 - move[1]) + move[2]),
    )
    targets = [ys[dy] + xs[dx] + cores[dc] for dy, dx, dc in moves]
    sources = [ys[-dy] + xs[-dx] + cores[dc] for dy, dx, dc in moves]

    def block_copy(src, dst):
        return pltpu.make_async_remote_copy(
            src_ref=send.at[dst], dst_ref=recv.at[src],
            send_sem=send_sem.at[dst], recv_sem=recv_sem.at[src],
            device_id={"acq": dst}, device_id_type=MESH,
        )

    @pl.when(me == root)
    def _():
        pl.semaphore_wait(join_sem, peers - 1)
        lax.fori_loop(1, peers, let_go, 0)

    @pl.when(me != root)
    def _():
        pl.semaphore_wait(go_sem, 1)

    blocks_out = [block_copy(me, dst) for dst in targets]
    blocks_in = [block_copy(src, src) for src in sources]
    for copy in blocks_out:
        copy.start()
    for copy in blocks_in[::-1]:
        copy.wait_recv()

    count = peers * 8
    straight, crossed = [], []
    for i in range(peers):
        block = recv[i].astype(f32)
        near, far, rest = block[:8], block[8:16], block[16:]
        re = [jnp.where(sub < acqs, part, 0.0) for part in (near, far)]
        im = [
            jnp.where(sub < 4, part, jnp.where(sub < acqs, pltpu.roll(late, 6, 0), 0.0))
            for part, late in ((rest, near), (pltpu.roll(rest, 4, 0), far))
        ]
        straight.append(jnp.concatenate(re + im, axis=1))
        crossed.append(jnp.concatenate(im + [-part for part in re], axis=1))
    straight = jnp.concatenate(straight, axis=0)
    crossed = jnp.concatenate(crossed, axis=0)
    wide = lax.broadcasted_iota(jnp.int32, (8, 2 * RING), 1)
    spot = lax.rem((wide & (RING - 1)) - BLOCK * me + 4 * RING, RING).astype(f32)
    in_row = spot - BLOCK * jnp.floor((spot + 0.5) * (1.0 / BLOCK))
    used = spot < BLOCK * ROWS
    first = jnp.where(used & (in_row < PATCH), 1.0, 0.0)[:1]
    second = jnp.where(used & (in_row >= PATCH), 1.0, 0.0)[:1]
    lhs_ref[0 * count : 1 * count] = (straight * first).astype(bf16)
    lhs_ref[1 * count : 2 * count] = (crossed * first).astype(bf16)
    lhs_ref[2 * count : 3 * count] = (straight * second).astype(bf16)
    lhs_ref[3 * count : 4 * count] = (crossed * second).astype(bf16)
    gram[...] = lax.dot_general(
        lhs_ref[...], straight.astype(bf16), (((1,), (1,)), ((), ())), preferred_element_type=f32
    )

    groups = peers
    norm = 2.0 * peers * acqs
    both = (0, 1)

    def load(p, part, at):
        return gram[pl.ds((2 * p + part) * count + at, 8), :]

    def twice(value):
        return jnp.concatenate([value] * (count // 128), axis=1)

    def diagonal(g, totals, half):
        at = pl.multiple_of(g * 8, 8)
        new = []
        for p in both:
            mine = jnp.where(
                lane == sub + (at - 128 * half), load(p, 0, at)[:, 128 * half : 128 * half + 128], 0.0
            )
            power = jnp.sum(mine, axis=1, keepdims=True) / (PATCH * PATCH) + 1e-06
            column[p, 0, pl.ds(at, 8), :] = jnp.broadcast_to(lax.rsqrt(power) / PATCH, (8, 128))
            new.append(totals[p] + mine)
        return tuple(new)

    scale_rows = [[], []]
    for half in range(count // 128):
        totals = lax.fori_loop(
            16 * half, 16 * half + 16, functools.partial(diagonal, half=half),
            (jnp.zeros((8, 128), f32),) * 2, unroll=8,
        )
        for p in both:
            power = jnp.sum(totals[p], axis=0, keepdims=True) / (PATCH * PATCH) + 1e-06
            scale_rows[p].append(lax.rsqrt(power) / PATCH)
    scale_rows = [jnp.concatenate(rows, axis=1) for rows in scale_rows]

    def by_columns(g, totals, first):
        at = pl.multiple_of(g * 8, 8)
        new = []
        for p in both:
            tr, ti = totals[p]
            gr, gi = load(p, 0, at), load(p, 1, at)
            if first:
                scale = twice(column[p, 0, pl.ds(at, 8), :])
                new.append((tr + gr * scale, ti - gi * scale))
            else:
                ur = twice(column[p, 1, pl.ds(at, 8), :])
                ui = twice(column[p, 2, pl.ds(at, 8), :])
                new.append((tr + (gr * ur + gi * ui), ti + (gr * ui - gi * ur)))
        return tuple(new)

    def by_rows(g, totals, vectors, last):
        at = pl.multiple_of(g * 8, 8)
        new = []
        for p in both:
            ur, ui = vectors[p]
            gr, gi = load(p, 0, at), load(p, 1, at)
            scale = column[p, 0, pl.ds(at, 8), :]
            wr = jnp.sum(gr * ur - gi * ui, axis=1, keepdims=True) * scale
            wi = jnp.sum(gr * ui + gi * ur, axis=1, keepdims=True) * scale
            column[p, 1, pl.ds(at, 8), :] = wr if last else wr * scale
            column[p, 2, pl.ds(at, 8), :] = wi if last else wi * scale
            new.append(totals[p] + (wr * wr + wi * wi))
        return tuple(new)

    inverses = [None, None]
    for step in range(0, ITERS, 2):
        zero = jnp.zeros((8, count), f32)
        totals = lax.fori_loop(
            0, groups, functools.partial(by_columns, first=step == 0), ((zero, zero),) * 2, unroll=16
        )
        vectors = []
        for p in both:
            scale = scale_rows[p] if step == 0 else scale_rows[p] * inverses[p][:, :1]
            wr = jnp.sum(totals[p][0], axis=0, keepdims=True) * scale
            wi = jnp.sum(totals[p][1], axis=0, keepdims=True) * scale
            power = jnp.sum(wr * wr + wi * wi, axis=1, keepdims=True)
            scale = lax.rsqrt(power / norm + 1e-06) * scale_rows[p]
            vectors.append(tuple(jnp.broadcast_to(w * scale, (8, count)) for w in (wr, wi)))
        totals = lax.fori_loop(
            0, groups, functools.partial(by_rows, vectors=vectors, last=step + 2 == ITERS),
            (jnp.zeros((8, 128), f32),) * 2, unroll=16,
        )
        for p in both:
            power = jnp.sum(totals[p], axis=0, keepdims=True)
            inverses[p] = lax.rsqrt(power / norm + 1e-06)

    choice = lane >> 3
    factor = jnp.where((lane & 7) == sub, jnp.where(choice < 2, inverses[0], inverses[1]), 0.0)
    factor = jnp.where(choice < 4, factor, 0.0)

    def message(g, carry):
        at = pl.multiple_of(g * 8, 8)
        re = jnp.where(choice < 2, column[0, 1, pl.ds(at, 8), :], column[1, 1, pl.ds(at, 8), :])
        im = jnp.where(choice < 2, column[0, 2, pl.ds(at, 8), :], column[1, 2, pl.ds(at, 8), :])
        value = jnp.where((choice & 1) == 0, re, im) * factor
        back_send[g] = jnp.sum(value, axis=0, keepdims=True)
        return carry

    lax.fori_loop(0, groups, message, 0, unroll=16)
    back_recv[me] = back_send[me]

    def back_copy(src, dst):
        return pltpu.make_async_remote_copy(
            src_ref=back_send.at[dst], dst_ref=back_recv.at[src],
            send_sem=back_send_sem.at[dst], recv_sem=back_recv_sem.at[src],
            device_id={"acq": dst}, device_id_type=MESH,
        )

    backs_out = [back_copy(me, dst) for dst in targets]
    backs_in = [back_copy(src, src) for src in sources]
    for copy in backs_out:
        copy.start()
    for copy in blocks_out:
        copy.wait_send()
    for copy in backs_in[::-1]:
        copy.wait_recv()

    values = back_recv[...].reshape(peers, 128)
    into = lax.broadcasted_iota(jnp.int32, (peers, 2 * peers), 1)
    source = lax.broadcasted_iota(jnp.int32, (peers, 2 * peers), 0)
    result = jnp.zeros((16, 2 * peers), f32)
    for p in range(2):
        result = result + lax.dot_general(
            values[:, 16 * p : 16 * p + 16], (into == 2 * source + p).astype(f32),
            (((0,), (0,)), ((), ())), precision=lax.Precision.HIGHEST, preferred_element_type=f32,
        )
    for c in range(2):
        out_ref[c, :, 0, :] = result[8 * c : 8 * c + acqs]
    for copy in backs_out:
        copy.wait_send()

    @pl.when(has_down)
    def _():
        to_down.wait_send()

    @pl.when(has_up)
    def _():
        to_up.wait_send()


def on_device(images, pixel_shift, fraction_index):
    acqs = images.shape[1]
    peers = lax.axis_size("acq")
    bands = lax.axis_size("band")
    f32, bf16 = jnp.float32, jnp.bfloat16
    vmem = pl.BlockSpec(memory_space=pltpu.VMEM)
    dma = pltpu.SemaphoreType.DMA
    return pl.pallas_call(
        functools.partial(kernel, acqs, peers, bands),
        out_shape=jax.ShapeDtypeStruct((2, acqs, 1, 2 * peers), f32),
        in_specs=[vmem] * 4,
        out_specs=vmem,
        scratch_shapes=[
            pltpu.VMEM((2, 8, 128), jnp.int32),
            pltpu.VMEM((LOCAL, LANES), bf16),
            pltpu.VMEM((EDGE // 8, 8, images.shape[3]), bf16),
            pltpu.VMEM((EDGE // 8, 8, images.shape[3]), bf16),
            pltpu.VMEM((2 * ROWS * 8, 256), f32),
            pltpu.VMEM((2 * ROWS * 8, LANES), f32),
            pltpu.VMEM((ROWS, 16, LANES + 256), bf16),
            pltpu.VMEM(((LANES + 256) // 128, 16, 16, 128), bf16),
            pltpu.VMEM((peers, 24, 128), bf16),
            pltpu.VMEM((peers, 24, 128), bf16),
            pltpu.VMEM((4 * peers * 8, 2 * RING), bf16),
            pltpu.VMEM((4 * peers * 8, peers * 8), f32),
            pltpu.VMEM((2, 3, peers * 8, 128), f32),
            pltpu.VMEM((peers, 1, 128), f32),
            pltpu.VMEM((peers, 1, 128), f32),
            pltpu.SemaphoreType.REGULAR, pltpu.SemaphoreType.REGULAR,
            dma((2,)), dma((2,)),
            dma((peers,)), dma((peers,)),
            dma((peers,)), dma((peers,)),
        ],
        compiler_params=pltpu.CompilerParams(
            collective_id=0, has_side_effects=True, vmem_limit_bytes=48 * 1024 * 1024
        ),
    )(pixel_shift.T, fraction_index.T, jnp.asarray(index_rows(acqs)), images)


def solution(mesh):
    placed = (P(None, "acq", "band", None), P("acq", None), P("acq", None))
    return jax.shard_map(
        on_device,
        mesh=mesh,
        in_specs=placed,
        out_specs=P(None, "acq", "band", None),
        check_vma=False,
    )
```

```python
import functools

import jax
import jax.numpy as jnp
import numpy as np
from jax import lax
from jax.experimental import pallas as pl
from jax.experimental.pallas import tpu as pltpu
from jax.sharding import PartitionSpec as P

PATCH = 11
QUANT = 16
HALO = 7
ITERS = 4
MESH = pl.DeviceIdType.MESH

ROWS = 11
LANES = 768
WIDE = 896
ABOVE = 6
BELOW = 7


def tap_table():
    fraction = np.arange(QUANT, dtype=np.float64)[:, None] / QUANT
    where_at = np.arange(8, dtype=np.float64)[None, :] - 3.0 - fraction
    raw_taps = np.sinc(where_at) * (0.5 + 0.5 * np.cos(np.pi * where_at / 4.0))
    return (raw_taps / raw_taps.sum(axis=1, keepdims=True)).astype(np.float32)


def index_rows(acqs):
    rows = np.full((16, 256), -1, np.float32)
    for c in range(2):
        for a in range(acqs):
            for i in range(ROWS):
                k = (a * ROWS + i) * 2 + c
                rows[2, k], rows[3, k], rows[4, k] = a, i, c
            for t in range(ABOVE):
                k = (a * ABOVE + t) * 2 + c
                rows[5, k], rows[6, k], rows[7, k] = a, t - ABOVE, c
            for t in range(BELOW):
                k = 128 + (a * BELOW + t) * 2 + c
                rows[5, k], rows[6, k], rows[7, k] = a, ROWS + t, c
    rows[8, : QUANT * 8] = tap_table().reshape(-1)
    return rows


def kernel(
    acqs, peers, bands,
    shift_hbm, fraction_hbm, index_hbm, image_hbm, out_ref,
    shift_ref, fraction_ref, index_ref, image_ref, offsets, halo_top, halo_bottom, weight_ref, y_ref, z_ref, moved_ref,
    send, recv, lhs_ref, gram, column, back_send, back_recv,
    fetch_sem, join_sem, go_sem,
    halo_send_sem, halo_recv_sem, send_sem, recv_sem, back_send_sem, back_recv_sem,
):
    f32, bf16 = jnp.float32, jnp.bfloat16
    me = lax.axis_index("acq")
    band = lax.axis_index("band")
    has_up, has_down = band > 0, band < bands - 1
    down = lax.min(band + 1, bands - 1)
    up = lax.max(band - 1, 0)

    barrier = pltpu.get_barrier_semaphore()

    root = min(1, peers - 1)

    def greet(k, carry):
        pl.semaphore_signal(
            barrier, inc=1, device_id={"acq": lax.rem(me + k, peers)}, device_id_type=MESH
        )
        return carry

    def let_go(k, carry):
        pl.semaphore_signal(
            go_sem, inc=1, device_id={"acq": lax.rem(me + k, peers)}, device_id_type=MESH
        )
        return carry

    @pl.when(has_down)
    def _():
        pl.semaphore_signal(barrier, inc=1, device_id={"band": down}, device_id_type=MESH)

    @pl.when(has_up)
    def _():
        pl.semaphore_signal(barrier, inc=1, device_id={"band": up}, device_id_type=MESH)

    @pl.when(me == root)
    def _():
        lax.fori_loop(1, peers, greet, 0)

    fetches = [
        pltpu.make_async_copy(src, dst, fetch_sem.at[i])
        for i, (src, dst) in enumerate(
            ((image_hbm, image_ref), (index_hbm, index_ref), (shift_hbm, shift_ref),
             (fraction_hbm, fraction_ref))
        )
    ]
    for fetch in fetches:
        fetch.start()
    offsets[...] = jnp.zeros_like(offsets)
    for fetch in fetches:
        fetch.wait()
    cols = image_ref.shape[3]

    greeters = (
        has_up.astype(jnp.int32) + has_down.astype(jnp.int32) + (me != root).astype(jnp.int32)
    )
    pl.semaphore_wait(barrier, greeters)

    @pl.when(me != root)
    def _():
        pl.semaphore_signal(join_sem, inc=1, device_id={"acq": root}, device_id_type=MESH)

    to_down = pltpu.make_async_remote_copy(
        src_ref=image_ref.at[:, ROWS - ABOVE :], dst_ref=halo_top,
        send_sem=halo_send_sem.at[0], recv_sem=halo_recv_sem.at[0],
        device_id={"band": down}, device_id_type=MESH,
    )
    to_up = pltpu.make_async_remote_copy(
        src_ref=image_ref.at[:, :BELOW], dst_ref=halo_bottom,
        send_sem=halo_send_sem.at[1], recv_sem=halo_recv_sem.at[1],
        device_id={"band": up}, device_id_type=MESH,
    )

    @pl.when(has_down)
    def _():
        to_down.start()

    @pl.when(has_up)
    def _():
        to_up.start()

    @pl.when(jnp.logical_not(has_up))
    def _():
        halo_top[...] = jnp.zeros_like(halo_top)

    @pl.when(jnp.logical_not(has_down))
    def _():
        halo_bottom[...] = jnp.zeros_like(halo_bottom)

    offsets[0, :2, :acqs] = shift_ref[...]
    offsets[1, :2, :acqs] = fraction_ref[...]
    lane = lax.broadcasted_iota(jnp.int32, (8, 128), 1)
    sub = lax.broadcasted_iota(jnp.int32, (8, 128), 0)

    held = (jnp.where(sub < acqs, sub, sub - 2), sub & 3)
    held_part = (jnp.where(sub < acqs, 0.0, 1.0), jnp.ones((8, 128), f32))

    def offset_weights(which, group):
        shift, fraction = (
            jnp.sum(
                jnp.where(lane == held[group], offsets[i, which : which + 1, :], 0),
                axis=1, keepdims=True,
            )
            for i in range(2)
        )
        taps = jnp.where((lane >> 3) == fraction, index_ref[8:9, :128], 0.0)
        for step in (8, 16, 32, 64):
            taps = taps + pltpu.roll(taps, step, 1)
        weights = []
        for off in range(1, 2 * HALO + 1):
            hit = (lane == off - (HALO - 3) - shift) & (lane < 8)
            weights.append(jnp.sum(jnp.where(hit, taps, 0.0), axis=1, keepdims=True))
        return weights

    row_weights = [offset_weights(0, group) for group in range(2)]
    col_weights = [offset_weights(1, group) for group in range(2)]

    def row_matrix(at):
        place = index_ref[at + 1 : at + 2, :]
        own = []
        for group in range(2):
            acq = jnp.concatenate([held[group].astype(f32)] * 2, axis=1)
            part = jnp.concatenate([held_part[group]] * 2, axis=1)
            own.append((index_ref[at : at + 1, :] == acq) & (index_ref[at + 2 : at + 3, :] == part))
        for r in range(ROWS):
            totals = [jnp.zeros((8, 256), f32)] * 2
            for off in range(1, 2 * HALO + 1):
                hit = place == float(off - HALO + r)
                for group in range(2):
                    totals[group] = jnp.where(hit, row_weights[group][off - 1], totals[group])
            for group in range(2):
                m = (r * 2 + group) * 8
                weight_ref[m : m + 8, :] = jnp.where(own[group], totals[group], 0.0)
        whole = weight_ref[...]
        high = whole.astype(bf16)
        low = (whole - high.astype(f32)).astype(bf16)
        return high, low

    def filtered(matrix, rows_ref, at):
        count = rows_ref.shape[0] * rows_ref.shape[1] * 2
        rows = rows_ref[...].reshape(count, cols)
        high, low = (half[:, at : at + count] for half in matrix)
        return jnp.dot(high, rows, preferred_element_type=f32) + jnp.dot(
            low, rows, preferred_element_type=f32
        )

    y_ref[:, LANES - 128 :] = jnp.zeros((ROWS * 16, 128), f32)
    y_ref[:, :cols] = filtered(row_matrix(2), image_ref, 0)
    matrix = row_matrix(5)

    @pl.when(has_up)
    def _():
        to_down.wait_recv()

    @pl.when(has_down)
    def _():
        to_up.wait_recv()

    y_ref[:, :cols] += filtered(matrix, halo_top, 0) + filtered(matrix, halo_bottom, 128)

    for r in range(ROWS):
        parts = []
        for group in range(2):
            m = (r * 2 + group) * 8
            y = y_ref[m : m + 8, :]
            moved = [y] + [pltpu.roll(y, LANES - low, 1) for low in range(1, 4)]
            z = None
            for high in range(4):
                total = None
                for low in range(4):
                    off = 4 * high + low
                    if 1 <= off <= 2 * HALO:
                        term = col_weights[group][off - 1] * moved[low]
                        total = term if total is None else total + term
                if 4 * high != 8:
                    total = pltpu.roll(total, (8 - 4 * high) % LANES, 1)
                z = total if z is None else z + total
            z = jnp.concatenate([z, jnp.zeros((8, WIDE - LANES), f32)], axis=1)
            parts.append(pltpu.roll(z, (PATCH * r + WIDE - 1) % WIDE, 1))
        z_ref[r] = jnp.concatenate(parts, axis=0).astype(bf16)

    def bits(v):
        place = lax.broadcasted_iota(jnp.int32, (16, 128), 1).astype(f32) + (128.0 * v + 0.5)
        rest = jnp.floor(place * (1.0 / PATCH))
        rest = rest - 16.0 * jnp.floor(rest * (1.0 / 16))
        found = []
        for bit in (8.0, 4.0, 2.0, 1.0):
            hit = jnp.where(rest >= bit, 1.0, 0.0)
            rest = rest - bit * hit
            found.append(hit.astype(bf16) > 0.5)
        return found[::-1]

    for v in range(WIDE // 128):
        rows = [z_ref[r, :, 128 * v : 128 * v + 128] for r in range(ROWS)]
        rows = rows + rows[: 16 - ROWS]
        for k, hit in enumerate(bits(v)):
            rows = [jnp.where(hit, rows[(i + (1 << k)) % 16], rows[i]) for i in range(16)]
        for i in range(16):
            moved_ref[v, i] = rows[i]

    narrow = lax.broadcasted_iota(jnp.int32, (16, 128), 1).astype(f32).astype(bf16)
    upper = lax.broadcasted_iota(jnp.int32, (16, 128), 0).astype(f32).astype(bf16) < 12.0
    for j in range(peers):
        halves = []
        for q in (2 * j, 2 * j + 1):
            v = PATCH * q // 128
            value = moved_ref[v, -q % 16]
            if PATCH * q + PATCH * ROWS > 128 * (v + 1):
                value = jnp.where(
                    narrow >= float(PATCH * q - 128 * v), value, moved_ref[v + 1, -q % 16]
                )
            halves.append(value)
        send[j, 0:8, :] = halves[0][:8]
        send[j, 8:16, :] = halves[1][:8]
        send[j, 16:24, :] = jnp.where(upper, halves[0], halves[1])[8:]

    recv[me] = send[me]

    ys = [lax.rem(me // 8 + d, 4) * 8 for d in range(4)]
    xs = [lax.rem(lax.rem(me // 2, 4) + d, 4) * 2 for d in range(4)]
    cores = [lax.rem(me, 2), 1 - lax.rem(me, 2)]
    moves = sorted(
        ((dy, dx, dc) for dy in range(4) for dx in range(4) for dc in range(2) if dy or dx or dc),
        key=lambda move: -(4 * min(move[0], 4 - move[0]) + 2 * min(move[1], 4 - move[1]) + move[2]),
    )
    targets = [ys[dy] + xs[dx] + cores[dc] for dy, dx, dc in moves]
    sources = [ys[-dy] + xs[-dx] + cores[dc] for dy, dx, dc in moves]

    def block_copy(src, dst):
        return pltpu.make_async_remote_copy(
            src_ref=send.at[dst], dst_ref=recv.at[src],
            send_sem=send_sem.at[dst], recv_sem=recv_sem.at[src],
            device_id={"acq": dst}, device_id_type=MESH,
        )

    @pl.when(me == root)
    def _():
        pl.semaphore_wait(join_sem, peers - 1)
        lax.fori_loop(1, peers, let_go, 0)

    @pl.when(me != root)
    def _():
        pl.semaphore_wait(go_sem, 1)

    blocks_out = [block_copy(me, dst) for dst in targets]
    blocks_in = [block_copy(src, src) for src in sources]
    for copy in blocks_out:
        copy.start()

    count = peers * 8
    used = []
    for p in range(2):
        spot = lax.rem(lane + (128 * peers - PATCH * p) - 2 * PATCH * me, 128)
        used.append((spot < PATCH * ROWS) & (sub < acqs))
    order = [me] + sources[::-1]
    waits = [None] + blocks_in[::-1]
    for i in range(0, peers, 2):
        straight, crossed = [[], []], [[], []]
        for k in (i, i + 1):
            if waits[k] is not None:
                waits[k].wait_recv()
            block = recv[order[k]].astype(f32)
            near, far, rest = block[:8], block[8:16], block[16:]
            for p, (re, im, late) in enumerate(
                ((near, rest, near), (far, pltpu.roll(rest, 4, 0), far))
            ):
                im = jnp.where(sub < 4, im, pltpu.roll(late, 6, 0))
                re, im = jnp.where(used[p], re, 0.0), jnp.where(used[p], im, 0.0)
                straight[p].append(jnp.concatenate([re, im], axis=1))
                crossed[p].append(jnp.concatenate([im, -re], axis=1))
        for p in range(2):
            lhs_ref[p, 8 * i : 8 * i + 16] = jnp.concatenate(straight[p], axis=0).astype(bf16)
            lhs_ref[p, count + 8 * i : count + 8 * i + 16] = jnp.concatenate(
                crossed[p], axis=0
            ).astype(bf16)
    for p in range(2):
        gram[2 * count * p : 2 * count * (p + 1)] = lax.dot_general(
            lhs_ref[p], lhs_ref[p, :count], (((1,), (1,)), ((), ())), preferred_element_type=f32
        )

    groups = peers
    norm = 2.0 * peers * acqs
    both = (0, 1)

    def load(p, part, at):
        return gram[pl.ds((2 * p + part) * count + at, 8), :]

    def twice(value):
        return jnp.concatenate([value] * (count // 128), axis=1)

    def diagonal(g, totals, half):
        at = pl.multiple_of(g * 8, 8)
        new = []
        for p in both:
            mine = jnp.where(
                lane == sub + (at - 128 * half), load(p, 0, at)[:, 128 * half : 128 * half + 128], 0.0
            )
            power = jnp.sum(mine, axis=1, keepdims=True) / (PATCH * PATCH) + 1e-06
            column[p, 0, pl.ds(at, 8), :] = jnp.broadcast_to(lax.rsqrt(power) / PATCH, (8, 128))
            new.append(totals[p] + mine)
        return tuple(new)

    scale_rows = [[], []]
    for half in range(count // 128):
        totals = lax.fori_loop(
            16 * half, 16 * half + 16, functools.partial(diagonal, half=half),
            (jnp.zeros((8, 128), f32),) * 2, unroll=8,
        )
        for p in both:
            power = jnp.sum(totals[p], axis=0, keepdims=True) / (PATCH * PATCH) + 1e-06
            scale_rows[p].append(lax.rsqrt(power) / PATCH)
    scale_rows = [jnp.concatenate(rows, axis=1) for rows in scale_rows]

    def by_columns(g, totals, first):
        at = pl.multiple_of(g * 8, 8)
        new = []
        for p in both:
            tr, ti = totals[p]
            gr, gi = load(p, 0, at), load(p, 1, at)
            if first:
                scale = twice(column[p, 0, pl.ds(at, 8), :])
                new.append((tr + gr * scale, ti - gi * scale))
            else:
                ur = twice(column[p, 1, pl.ds(at, 8), :])
                ui = twice(column[p, 2, pl.ds(at, 8), :])
                new.append((tr + (gr * ur + gi * ui), ti + (gr * ui - gi * ur)))
        return tuple(new)

    def by_rows(g, totals, vectors, last):
        at = pl.multiple_of(g * 8, 8)
        new = []
        for p in both:
            ur, ui = vectors[p]
            gr, gi = load(p, 0, at), load(p, 1, at)
            scale = column[p, 0, pl.ds(at, 8), :]
            wr = jnp.sum(gr * ur - gi * ui, axis=1, keepdims=True) * scale
            wi = jnp.sum(gr * ui + gi * ur, axis=1, keepdims=True) * scale
            column[p, 1, pl.ds(at, 8), :] = wr if last else wr * scale
            column[p, 2, pl.ds(at, 8), :] = wi if last else wi * scale
            new.append(totals[p] + (wr * wr + wi * wi))
        return tuple(new)

    inverses = [None, None]
    for step in range(0, ITERS, 2):
        zero = jnp.zeros((8, count), f32)
        totals = lax.fori_loop(
            0, groups, functools.partial(by_columns, first=step == 0), ((zero, zero),) * 2, unroll=16
        )
        vectors = []
        for p in both:
            scale = scale_rows[p] if step == 0 else scale_rows[p] * inverses[p][:, :1]
            wr = jnp.sum(totals[p][0], axis=0, keepdims=True) * scale
            wi = jnp.sum(totals[p][1], axis=0, keepdims=True) * scale
            power = jnp.sum(wr * wr + wi * wi, axis=1, keepdims=True)
            scale = lax.rsqrt(power / norm + 1e-06) * scale_rows[p]
            vectors.append(tuple(jnp.broadcast_to(w * scale, (8, count)) for w in (wr, wi)))
        totals = lax.fori_loop(
            0, groups, functools.partial(by_rows, vectors=vectors, last=step + 2 == ITERS),
            (jnp.zeros((8, 128), f32),) * 2, unroll=16,
        )
        for p in both:
            power = jnp.sum(totals[p], axis=0, keepdims=True)
            inverses[p] = lax.rsqrt(power / norm + 1e-06)

    choice = lane >> 3
    factor = jnp.where((lane & 7) == sub, jnp.where(choice < 2, inverses[0], inverses[1]), 0.0)
    factor = jnp.where(choice < 4, factor, 0.0)

    def message(g, carry):
        at = pl.multiple_of(g * 8, 8)
        re = jnp.where(choice < 2, column[0, 1, pl.ds(at, 8), :], column[1, 1, pl.ds(at, 8), :])
        im = jnp.where(choice < 2, column[0, 2, pl.ds(at, 8), :], column[1, 2, pl.ds(at, 8), :])
        value = jnp.where((choice & 1) == 0, re, im) * factor
        back_send[g] = jnp.sum(value, axis=0, keepdims=True)
        return carry

    lax.fori_loop(0, groups, message, 0, unroll=16)
    back_recv[me] = back_send[0]

    def back_copy(src, dst, group):
        return pltpu.make_async_remote_copy(
            src_ref=back_send.at[group], dst_ref=back_recv.at[src],
            send_sem=back_send_sem.at[dst], recv_sem=back_recv_sem.at[src],
            device_id={"acq": dst}, device_id_type=MESH,
        )

    backs_out = [back_copy(me, order[g], g) for g in range(peers - 1, 0, -1)]
    backs_in = [back_copy(src, src, 0) for src in targets]
    for copy in backs_out:
        copy.start()
    for copy in blocks_out:
        copy.wait_send()
    for copy in backs_in[::-1]:
        copy.wait_recv()

    values = back_recv[...].reshape(peers, 128)
    into = lax.broadcasted_iota(jnp.int32, (peers, 2 * peers), 1)
    source = lax.broadcasted_iota(jnp.int32, (peers, 2 * peers), 0)
    result = jnp.zeros((16, 2 * peers), f32)
    for p in range(2):
        result = result + lax.dot_general(
            values[:, 16 * p : 16 * p + 16], (into == 2 * source + p).astype(f32),
            (((0,), (0,)), ((), ())), precision=lax.Precision.HIGHEST, preferred_element_type=f32,
        )
    for c in range(2):
        out_ref[c, :, 0, :] = result[8 * c : 8 * c + acqs]
    for copy in backs_out:
        copy.wait_send()

    @pl.when(has_down)
    def _():
        to_down.wait_send()

    @pl.when(has_up)
    def _():
        to_up.wait_send()


def on_device(images, pixel_shift, fraction_index):
    acqs = images.shape[1]
    peers = lax.axis_size("acq")
    bands = lax.axis_size("band")
    f32, bf16 = jnp.float32, jnp.bfloat16
    vmem = pl.BlockSpec(memory_space=pltpu.VMEM)
    dma = pltpu.SemaphoreType.DMA
    return pl.pallas_call(
        functools.partial(kernel, acqs, peers, bands),
        out_shape=pltpu.VMEM((2, acqs, 1, 2 * peers), f32),
        in_specs=[pl.BlockSpec(memory_space=pl.ANY)] * 4,
        out_specs=vmem,
        scratch_shapes=[
            pltpu.VMEM((2, acqs), jnp.int32),
            pltpu.VMEM((2, acqs), jnp.int32),
            pltpu.VMEM((16, 256), f32),
            pltpu.VMEM((acqs, ROWS, 2, images.shape[3]), bf16),
            pltpu.VMEM((2, 8, 128), jnp.int32),
            pltpu.VMEM((acqs, ABOVE, 2, images.shape[3]), bf16),
            pltpu.VMEM((acqs, BELOW, 2, images.shape[3]), bf16),
            pltpu.VMEM((2 * ROWS * 8, 256), f32),
            pltpu.VMEM((2 * ROWS * 8, LANES), f32),
            pltpu.VMEM((ROWS, 16, WIDE), bf16),
            pltpu.VMEM((WIDE // 128, 16, 16, 128), bf16),
            pltpu.VMEM((peers, 24, 128), bf16),
            pltpu.VMEM((peers, 24, 128), bf16),
            pltpu.VMEM((2, 2 * peers * 8, 256), bf16),
            pltpu.VMEM((4 * peers * 8, peers * 8), f32),
            pltpu.VMEM((2, 3, peers * 8, 128), f32),
            pltpu.VMEM((peers, 1, 128), f32),
            pltpu.VMEM((peers, 1, 128), f32),
            dma((4,)), pltpu.SemaphoreType.REGULAR, pltpu.SemaphoreType.REGULAR,
            dma((2,)), dma((2,)),
            dma((peers,)), dma((peers,)),
            dma((peers,)), dma((peers,)),
        ],
        compiler_params=pltpu.CompilerParams(
            collective_id=0, has_side_effects=True, vmem_limit_bytes=60 * 1024 * 1024
        ),
    )(*(
        pltpu.with_memory_space_constraint(operand, pltpu.HBM)
        for operand in (
            pixel_shift.T, fraction_index.T, jnp.asarray(index_rows(acqs)),
            jnp.transpose(images, (1, 2, 0, 3)),
        )
    ))


def solution(mesh):
    placed = (P(None, "acq", "band", None), P("acq", None), P("acq", None))
    return jax.shard_map(
        on_device,
        mesh=mesh,
        in_specs=placed,
        out_specs=P(None, "acq", "band", None),
        check_vma=False,
    )
```

```python
import functools

import jax
import jax.numpy as jnp
import numpy as np
from jax import lax
from jax.experimental import pallas as pl
from jax.experimental.pallas import tpu as pltpu
from jax.sharding import PartitionSpec as P

PATCH = 11
QUANT = 16
HALO = 7
ITERS = 4
MESH = pl.DeviceIdType.MESH

ROWS = 11
LANES = 768
WIDE = 896
ABOVE = 6
BELOW = 7


def tap_table():
    fraction = np.arange(QUANT, dtype=np.float64)[:, None] / QUANT
    where_at = np.arange(8, dtype=np.float64)[None, :] - 3.0 - fraction
    raw_taps = np.sinc(where_at) * (0.5 + 0.5 * np.cos(np.pi * where_at / 4.0))
    return (raw_taps / raw_taps.sum(axis=1, keepdims=True)).astype(np.float32)


def index_rows(acqs):
    rows = np.full((16, 256), -1, np.float32)
    for c in range(2):
        for a in range(acqs):
            for i in range(ROWS):
                k = (a * ROWS + i) * 2 + c
                rows[2, k], rows[3, k], rows[4, k] = a, i, c
            for t in range(ABOVE):
                k = (a * ABOVE + t) * 2 + c
                rows[5, k], rows[6, k], rows[7, k] = a, t - ABOVE, c
            for t in range(BELOW):
                k = 128 + (a * BELOW + t) * 2 + c
                rows[5, k], rows[6, k], rows[7, k] = a, ROWS + t, c
    rows[8, : QUANT * 8] = tap_table().reshape(-1)
    return rows


def kernel(
    acqs, peers, bands,
    shift_hbm, fraction_hbm, index_hbm, image_hbm, out_ref,
    shift_ref, fraction_ref, index_ref, image_ref, offsets, halo_top, halo_bottom, weight_ref, y_ref, z_ref, moved_ref,
    send, recv, lhs_ref, gram, column, back_send, back_recv,
    fetch_sem, join_sem, go_sem,
    halo_send_sem, halo_recv_sem, send_sem, recv_sem, back_send_sem, back_recv_sem,
):
    f32, bf16 = jnp.float32, jnp.bfloat16
    me = lax.axis_index("acq")
    band = lax.axis_index("band")
    has_up, has_down = band > 0, band < bands - 1
    down = lax.min(band + 1, bands - 1)
    up = lax.max(band - 1, 0)

    barrier = pltpu.get_barrier_semaphore()

    root = min(1, peers - 1)

    def greet(k, carry):
        pl.semaphore_signal(
            barrier, inc=1, device_id={"acq": lax.rem(me + k, peers)}, device_id_type=MESH
        )
        return carry

    def let_go(k, carry):
        pl.semaphore_signal(
            go_sem, inc=1, device_id={"acq": lax.rem(me + k, peers)}, device_id_type=MESH
        )
        return carry

    @pl.when(has_down)
    def _():
        pl.semaphore_signal(barrier, inc=1, device_id={"band": down}, device_id_type=MESH)

    @pl.when(has_up)
    def _():
        pl.semaphore_signal(barrier, inc=1, device_id={"band": up}, device_id_type=MESH)

    @pl.when(me == root)
    def _():
        lax.fori_loop(1, peers, greet, 0)

    fetches = [
        pltpu.make_async_copy(src, dst, fetch_sem.at[i])
        for i, (src, dst) in enumerate(
            ((image_hbm, image_ref), (index_hbm, index_ref), (shift_hbm, shift_ref),
             (fraction_hbm, fraction_ref))
        )
    ]
    for fetch in fetches:
        fetch.start()
    cols = image_ref.shape[3]
    greeters = (
        has_up.astype(jnp.int32) + has_down.astype(jnp.int32) + (me != root).astype(jnp.int32)
    )
    pl.semaphore_wait(barrier, greeters)

    @pl.when(me != root)
    def _():
        pl.semaphore_signal(join_sem, inc=1, device_id={"acq": root}, device_id_type=MESH)

    to_down = pltpu.make_async_remote_copy(
        src_ref=image_hbm.at[:, ROWS - ABOVE :], dst_ref=halo_top,
        send_sem=halo_send_sem.at[0], recv_sem=halo_recv_sem.at[0],
        device_id={"band": down}, device_id_type=MESH,
    )
    to_up = pltpu.make_async_remote_copy(
        src_ref=image_hbm.at[:, :BELOW], dst_ref=halo_bottom,
        send_sem=halo_send_sem.at[1], recv_sem=halo_recv_sem.at[1],
        device_id={"band": up}, device_id_type=MESH,
    )

    @pl.when(has_down)
    def _():
        to_down.start()

    @pl.when(has_up)
    def _():
        to_up.start()

    @pl.when(jnp.logical_not(has_up))
    def _():
        halo_top[...] = jnp.zeros_like(halo_top)

    @pl.when(jnp.logical_not(has_down))
    def _():
        halo_bottom[...] = jnp.zeros_like(halo_bottom)

    offsets[...] = jnp.zeros_like(offsets)
    for fetch in fetches:
        fetch.wait()
    offsets[0, :2, :acqs] = shift_ref[...]
    offsets[1, :2, :acqs] = fraction_ref[...]
    lane = lax.broadcasted_iota(jnp.int32, (8, 128), 1)
    sub = lax.broadcasted_iota(jnp.int32, (8, 128), 0)

    held = (jnp.where(sub < acqs, sub, sub - 2), sub & 3)
    held_part = (jnp.where(sub < acqs, 0.0, 1.0), jnp.ones((8, 128), f32))

    def offset_weights(which, group):
        shift, fraction = (
            jnp.sum(
                jnp.where(lane == held[group], offsets[i, which : which + 1, :], 0),
                axis=1, keepdims=True,
            )
            for i in range(2)
        )
        taps = jnp.where((lane >> 3) == fraction, index_ref[8:9, :128], 0.0)
        for step in (8, 16, 32, 64):
            taps = taps + pltpu.roll(taps, step, 1)
        weights = []
        for off in range(1, 2 * HALO + 1):
            hit = (lane == off - (HALO - 3) - shift) & (lane < 8)
            weights.append(jnp.sum(jnp.where(hit, taps, 0.0), axis=1, keepdims=True))
        return weights

    row_weights = [offset_weights(0, group) for group in range(2)]
    col_weights = [offset_weights(1, group) for group in range(2)]

    def row_matrix(at):
        place = index_ref[at + 1 : at + 2, :]
        own = []
        for group in range(2):
            acq = jnp.concatenate([held[group].astype(f32)] * 2, axis=1)
            part = jnp.concatenate([held_part[group]] * 2, axis=1)
            own.append((index_ref[at : at + 1, :] == acq) & (index_ref[at + 2 : at + 3, :] == part))
        for r in range(ROWS):
            totals = [jnp.zeros((8, 256), f32)] * 2
            for off in range(1, 2 * HALO + 1):
                hit = place == float(off - HALO + r)
                for group in range(2):
                    totals[group] = jnp.where(hit, row_weights[group][off - 1], totals[group])
            for group in range(2):
                m = (r * 2 + group) * 8
                weight_ref[m : m + 8, :] = jnp.where(own[group], totals[group], 0.0)
        whole = weight_ref[...]
        high = whole.astype(bf16)
        low = (whole - high.astype(f32)).astype(bf16)
        return high, low

    def filtered(matrix, rows_ref, at):
        count = rows_ref.shape[0] * rows_ref.shape[1] * 2
        rows = rows_ref[...].reshape(count, cols)
        high, low = (half[:, at : at + count] for half in matrix)
        return jnp.dot(high, rows, preferred_element_type=f32) + jnp.dot(
            low, rows, preferred_element_type=f32
        )

    y_ref[:, LANES - 128 :] = jnp.zeros((ROWS * 16, 128), f32)
    y_ref[:, :cols] = filtered(row_matrix(2), image_ref, 0)
    matrix = row_matrix(5)

    @pl.when(has_up)
    def _():
        to_down.wait_recv()

    @pl.when(has_down)
    def _():
        to_up.wait_recv()

    y_ref[:, :cols] += filtered(matrix, halo_top, 0) + filtered(matrix, halo_bottom, 128)

    for r in range(ROWS):
        parts = []
        for group in range(2):
            m = (r * 2 + group) * 8
            y = y_ref[m : m + 8, :]
            moved = [y] + [pltpu.roll(y, LANES - low, 1) for low in range(1, 4)]
            z = None
            for high in range(4):
                total = None
                for low in range(4):
                    off = 4 * high + low
                    if 1 <= off <= 2 * HALO:
                        term = col_weights[group][off - 1] * moved[low]
                        total = term if total is None else total + term
                if 4 * high != 8:
                    total = pltpu.roll(total, (8 - 4 * high) % LANES, 1)
                z = total if z is None else z + total
            z = jnp.concatenate([z, jnp.zeros((8, WIDE - LANES), f32)], axis=1)
            parts.append(pltpu.roll(z, (PATCH * r + WIDE - 1) % WIDE, 1))
        z_ref[r] = jnp.concatenate(parts, axis=0).astype(bf16)

    def bits(v):
        place = lax.broadcasted_iota(jnp.int32, (16, 128), 1).astype(f32) + (128.0 * v + 0.5)
        rest = jnp.floor(place * (1.0 / PATCH))
        rest = rest - 16.0 * jnp.floor(rest * (1.0 / 16))
        found = []
        for bit in (8.0, 4.0, 2.0, 1.0):
            hit = jnp.where(rest >= bit, 1.0, 0.0)
            rest = rest - bit * hit
            found.append(hit.astype(bf16) > 0.5)
        return found[::-1]

    for v in range(WIDE // 128):
        rows = [z_ref[r, :, 128 * v : 128 * v + 128] for r in range(ROWS)]
        rows = rows + rows[: 16 - ROWS]
        for k, hit in enumerate(bits(v)):
            rows = [jnp.where(hit, rows[(i + (1 << k)) % 16], rows[i]) for i in range(16)]
        for i in range(16):
            moved_ref[v, i] = rows[i]

    narrow = lax.broadcasted_iota(jnp.int32, (16, 128), 1).astype(f32).astype(bf16)
    upper = lax.broadcasted_iota(jnp.int32, (16, 128), 0).astype(f32).astype(bf16) < 12.0
    for j in range(peers):
        halves = []
        for q in (2 * j, 2 * j + 1):
            v = PATCH * q // 128
            value = moved_ref[v, -q % 16]
            if PATCH * q + PATCH * ROWS > 128 * (v + 1):
                value = jnp.where(
                    narrow >= float(PATCH * q - 128 * v), value, moved_ref[v + 1, -q % 16]
                )
            halves.append(value)
        send[j, 0:8, :] = halves[0][:8]
        send[j, 8:16, :] = halves[1][:8]
        send[j, 16:24, :] = jnp.where(upper, halves[0], halves[1])[8:]

    recv[me] = send[me]

    ys = [lax.rem(me // 8 + d, 4) * 8 for d in range(4)]
    xs = [lax.rem(lax.rem(me // 2, 4) + d, 4) * 2 for d in range(4)]
    cores = [lax.rem(me, 2), 1 - lax.rem(me, 2)]
    moves = sorted(
        ((dy, dx, dc) for dy in range(4) for dx in range(4) for dc in range(2) if dy or dx or dc),
        key=lambda move: -(4 * min(move[0], 4 - move[0]) + 2 * min(move[1], 4 - move[1]) + move[2]),
    )
    targets = [ys[dy] + xs[dx] + cores[dc] for dy, dx, dc in moves]
    sources = [ys[-dy] + xs[-dx] + cores[dc] for dy, dx, dc in moves]

    def block_copy(src, dst):
        return pltpu.make_async_remote_copy(
            src_ref=send.at[dst], dst_ref=recv.at[src],
            send_sem=send_sem.at[dst], recv_sem=recv_sem.at[src],
            device_id={"acq": dst}, device_id_type=MESH,
        )

    @pl.when(me == root)
    def _():
        pl.semaphore_wait(join_sem, peers - 1)
        lax.fori_loop(1, peers, let_go, 0)

    @pl.when(me != root)
    def _():
        pl.semaphore_wait(go_sem, 1)

    blocks_out = [block_copy(me, dst) for dst in targets]
    blocks_in = [block_copy(src, src) for src in sources]
    for copy in blocks_out:
        copy.start()

    count = peers * 8
    used = []
    for p in range(2):
        spot = lax.rem(lane + (128 * peers - PATCH * p) - 2 * PATCH * me, 128)
        used.append((spot < PATCH * ROWS) & (sub < acqs))
    order = [me] + sources[::-1]
    waits = [None] + blocks_in[::-1]
    diagonals = [[jnp.zeros((8, 128), f32)] * (count // 128) for p in range(2)]
    for first, last in ((0, peers - 8), (peers - 8, peers)):
        straight, crossed = [[], []], [[], []]
        for k in range(first, last):
            if waits[k] is not None:
                waits[k].wait_recv()
        for k in range(first, last):
            block = recv[order[k]].astype(f32)
            near, far, rest = block[:8], block[8:16], block[16:]
            for p, (re, im, late) in enumerate(
                ((near, rest, near), (far, pltpu.roll(rest, 4, 0), far))
            ):
                im = jnp.where(sub < 4, im, pltpu.roll(late, 6, 0))
                re, im = jnp.where(used[p], re, 0.0), jnp.where(used[p], im, 0.0)
                power = jnp.sum(re * re + im * im, axis=1, keepdims=True) / (PATCH * PATCH) + 1e-06
                scale = jnp.broadcast_to(lax.rsqrt(power) / PATCH, (8, 128))
                column[p, 0, 8 * k : 8 * k + 8, :] = scale
                half, at = 8 * k // 128, 8 * k % 128
                diagonals[p][half] = jnp.where(lane == sub + at, scale, diagonals[p][half])
                straight[p].append(jnp.concatenate([re, im], axis=1))
                crossed[p].append(jnp.concatenate([im, -re], axis=1))
        for p in range(2):
            lhs_ref[p, 8 * first : 8 * last] = jnp.concatenate(straight[p], axis=0).astype(bf16)
            lhs_ref[p, count + 8 * first : count + 8 * last] = jnp.concatenate(
                crossed[p], axis=0
            ).astype(bf16)
    for p in range(2):
        gram[2 * count * p : 2 * count * (p + 1)] = lax.dot_general(
            lhs_ref[p], lhs_ref[p, :count], (((1,), (1,)), ((), ())), preferred_element_type=f32
        )

    groups = peers
    norm = 2.0 * peers * acqs
    both = (0, 1)

    def load(p, part, at):
        return gram[pl.ds((2 * p + part) * count + at, 8), :]

    def twice(value):
        return jnp.concatenate([value] * (count // 128), axis=1)

    scale_rows = [
        jnp.sum(jnp.concatenate(halves, axis=1), axis=0, keepdims=True) for halves in diagonals
    ]

    def by_columns(g, totals, first):
        at = pl.multiple_of(g * 8, 8)
        new = []
        for p in both:
            tr, ti = totals[p]
            gr, gi = load(p, 0, at), load(p, 1, at)
            if first:
                scale = twice(column[p, 0, pl.ds(at, 8), :])
                new.append((tr + gr * scale, ti - gi * scale))
            else:
                ur = twice(column[p, 1, pl.ds(at, 8), :])
                ui = twice(column[p, 2, pl.ds(at, 8), :])
                new.append((tr + (gr * ur + gi * ui), ti + (gr * ui - gi * ur)))
        return tuple(new)

    def by_rows(g, totals, vectors, last):
        at = pl.multiple_of(g * 8, 8)
        new = []
        for p in both:
            ur, ui = vectors[p]
            gr, gi = load(p, 0, at), load(p, 1, at)
            scale = column[p, 0, pl.ds(at, 8), :]
            wr = jnp.sum(gr * ur - gi * ui, axis=1, keepdims=True) * scale
            wi = jnp.sum(gr * ui + gi * ur, axis=1, keepdims=True) * scale
            column[p, 1, pl.ds(at, 8), :] = wr if last else wr * scale
            column[p, 2, pl.ds(at, 8), :] = wi if last else wi * scale
            new.append(totals[p] + (wr * wr + wi * wi))
        return tuple(new)

    inverses = [None, None]
    for step in range(0, ITERS, 2):
        zero = jnp.zeros((8, count), f32)
        totals = lax.fori_loop(
            0, groups, functools.partial(by_columns, first=step == 0), ((zero, zero),) * 2, unroll=32
        )
        vectors = []
        for p in both:
            scale = scale_rows[p] if step == 0 else scale_rows[p] * inverses[p][:, :1]
            wr = jnp.sum(totals[p][0], axis=0, keepdims=True) * scale
            wi = jnp.sum(totals[p][1], axis=0, keepdims=True) * scale
            power = jnp.sum(wr * wr + wi * wi, axis=1, keepdims=True)
            scale = lax.rsqrt(power / norm + 1e-06) * scale_rows[p]
            vectors.append(tuple(jnp.broadcast_to(w * scale, (8, count)) for w in (wr, wi)))
        totals = lax.fori_loop(
            0, groups, functools.partial(by_rows, vectors=vectors, last=step + 2 == ITERS),
            (jnp.zeros((8, 128), f32),) * 2, unroll=32,
        )
        for p in both:
            power = jnp.sum(totals[p], axis=0, keepdims=True)
            inverses[p] = lax.rsqrt(power / norm + 1e-06)

    choice = lane >> 3
    factor = jnp.where((lane & 7) == sub, jnp.where(choice < 2, inverses[0], inverses[1]), 0.0)
    factor = jnp.where(choice < 4, factor, 0.0)

    def back_copy(src, dst, group):
        return pltpu.make_async_remote_copy(
            src_ref=back_send.at[group], dst_ref=back_recv.at[src],
            send_sem=back_send_sem.at[dst], recv_sem=back_recv_sem.at[src],
            device_id={"acq": dst}, device_id_type=MESH,
        )

    backs_out = [back_copy(me, order[g], g) for g in range(peers - 1, 0, -1)]
    backs_in = [back_copy(src, src, 0) for src in targets]
    for g in range(peers - 1, -1, -1):
        rows = slice(8 * g, 8 * g + 8)
        re = jnp.where(choice < 2, column[0, 1, rows, :], column[1, 1, rows, :])
        im = jnp.where(choice < 2, column[0, 2, rows, :], column[1, 2, rows, :])
        value = jnp.where((choice & 1) == 0, re, im) * factor
        back_send[g] = jnp.sum(value, axis=0, keepdims=True)
        if g:
            backs_out[peers - 1 - g].start()
    back_recv[me] = back_send[0]
    for copy in blocks_out:
        copy.wait_send()
    for copy in backs_in[::-1]:
        copy.wait_recv()

    values = back_recv[...].reshape(peers, 128)
    into = lax.broadcasted_iota(jnp.int32, (peers, 4 * peers), 1)
    source = lax.broadcasted_iota(jnp.int32, (peers, 4 * peers), 0)
    into = into - jnp.where(into < 2 * peers, 0, 2 * peers + 1)
    result = lax.dot_general(
        values[:, :32], (into == 2 * source).astype(f32),
        (((0,), (0,)), ((), ())), precision=lax.Precision.HIGHEST, preferred_element_type=f32,
    )
    result = result[:16, : 2 * peers] + pltpu.roll(result[16:], 2 * peers, 1)[:, : 2 * peers]
    for c in range(2):
        out_ref[c, :, 0, :] = result[8 * c : 8 * c + acqs]
    for copy in backs_out:
        copy.wait_send()

    @pl.when(has_down)
    def _():
        to_down.wait_send()

    @pl.when(has_up)
    def _():
        to_up.wait_send()


def on_device(images, pixel_shift, fraction_index):
    acqs = images.shape[1]
    peers = lax.axis_size("acq")
    bands = lax.axis_size("band")
    f32, bf16 = jnp.float32, jnp.bfloat16
    vmem = pl.BlockSpec(memory_space=pltpu.VMEM)
    dma = pltpu.SemaphoreType.DMA
    return pl.pallas_call(
        functools.partial(kernel, acqs, peers, bands),
        out_shape=pltpu.VMEM((2, acqs, 1, 2 * peers), f32),
        in_specs=[pl.BlockSpec(memory_space=pl.ANY)] * 4,
        out_specs=vmem,
        scratch_shapes=[
            pltpu.VMEM((2, acqs), jnp.int32),
            pltpu.VMEM((2, acqs), jnp.int32),
            pltpu.VMEM((16, 256), f32),
            pltpu.VMEM((acqs, ROWS, 2, images.shape[3]), bf16),
            pltpu.VMEM((2, 8, 128), jnp.int32),
            pltpu.VMEM((acqs, ABOVE, 2, images.shape[3]), bf16),
            pltpu.VMEM((acqs, BELOW, 2, images.shape[3]), bf16),
            pltpu.VMEM((2 * ROWS * 8, 256), f32),
            pltpu.VMEM((2 * ROWS * 8, LANES), f32),
            pltpu.VMEM((ROWS, 16, WIDE), bf16),
            pltpu.VMEM((WIDE // 128, 16, 16, 128), bf16),
            pltpu.VMEM((peers, 24, 128), bf16),
            pltpu.VMEM((peers, 24, 128), bf16),
            pltpu.VMEM((2, 2 * peers * 8, 256), bf16),
            pltpu.VMEM((4 * peers * 8, peers * 8), f32),
            pltpu.VMEM((2, 3, peers * 8, 128), f32),
            pltpu.VMEM((peers, 1, 128), f32),
            pltpu.VMEM((peers, 1, 128), f32),
            dma((4,)), pltpu.SemaphoreType.REGULAR, pltpu.SemaphoreType.REGULAR,
            dma((2,)), dma((2,)),
            dma((peers,)), dma((peers,)),
            dma((peers,)), dma((peers,)),
        ],
        compiler_params=pltpu.CompilerParams(
            collective_id=0, has_side_effects=True, vmem_limit_bytes=60 * 1024 * 1024
        ),
    )(*(
        pltpu.with_memory_space_constraint(operand, pltpu.HBM)
        for operand in (
            pixel_shift.T, fraction_index.T, jnp.asarray(index_rows(acqs)),
            jnp.transpose(images, (1, 2, 0, 3)),
        )
    ))


def solution(mesh):
    placed = (P(None, "acq", "band", None), P("acq", None), P("acq", None))
    return jax.shard_map(
        on_device,
        mesh=mesh,
        in_specs=placed,
        out_specs=P(None, "acq", "band", None),
        check_vma=False,
    )
```

```python
import functools

import jax
import jax.numpy as jnp
import numpy as np
from jax import lax
from jax.experimental import pallas as pl
from jax.experimental.pallas import tpu as pltpu
from jax.sharding import PartitionSpec as P

PATCH = 11
QUANT = 16
HALO = 7
ITERS = 4
MESH = pl.DeviceIdType.MESH

ROWS = 11
LANES = 768
WIDE = 896
ABOVE = 6
BELOW = 7


def tap_table():
    fraction = np.arange(QUANT, dtype=np.float64)[:, None] / QUANT
    where_at = np.arange(8, dtype=np.float64)[None, :] - 3.0 - fraction
    raw_taps = np.sinc(where_at) * (0.5 + 0.5 * np.cos(np.pi * where_at / 4.0))
    return (raw_taps / raw_taps.sum(axis=1, keepdims=True)).astype(np.float32)


def index_rows(acqs):
    rows = np.full((16, 256), -1, np.float32)
    for c in range(2):
        for a in range(acqs):
            for i in range(ROWS):
                k = (a * ROWS + i) * 2 + c
                rows[2, k], rows[3, k], rows[4, k] = a, i, c
            for t in range(ABOVE):
                k = (a * ABOVE + t) * 2 + c
                rows[5, k], rows[6, k], rows[7, k] = a, t - ABOVE, c
            for t in range(BELOW):
                k = 128 + (a * BELOW + t) * 2 + c
                rows[5, k], rows[6, k], rows[7, k] = a, ROWS + t, c
    rows[8, : QUANT * 8] = tap_table().reshape(-1)
    return rows


def kernel(
    acqs, peers, bands,
    shift_hbm, fraction_hbm, index_hbm, image_hbm, out_ref,
    shift_ref, fraction_ref, index_ref, image_ref, offsets, halo_top, halo_bottom, weight_ref, y_ref, z_ref, moved_ref, bit_ref,
    send, recv, lhs_ref, gram, column, back_send, back_recv,
    fetch_sem, join_sem, go_sem,
    halo_send_sem, halo_recv_sem, send_sem, recv_sem, back_send_sem, back_recv_sem,
):
    f32, bf16 = jnp.float32, jnp.bfloat16
    me = lax.axis_index("acq")
    band = lax.axis_index("band")
    has_up, has_down = band > 0, band < bands - 1
    down = lax.min(band + 1, bands - 1)
    up = lax.max(band - 1, 0)

    barrier = pltpu.get_barrier_semaphore()

    root = min(1, peers - 1)

    def greet(k, carry):
        pl.semaphore_signal(
            barrier, inc=1, device_id={"acq": lax.rem(me + k, peers)}, device_id_type=MESH
        )
        return carry

    def let_go(k, carry):
        pl.semaphore_signal(
            go_sem, inc=1, device_id={"acq": lax.rem(me + k, peers)}, device_id_type=MESH
        )
        return carry

    @pl.when(has_down)
    def _():
        pl.semaphore_signal(barrier, inc=1, device_id={"band": down}, device_id_type=MESH)

    @pl.when(has_up)
    def _():
        pl.semaphore_signal(barrier, inc=1, device_id={"band": up}, device_id_type=MESH)

    @pl.when(me == root)
    def _():
        lax.fori_loop(1, peers, greet, 0)

    fetches = [
        pltpu.make_async_copy(src, dst, fetch_sem.at[i])
        for i, (src, dst) in enumerate(
            ((image_hbm, image_ref), (index_hbm, index_ref), (shift_hbm, shift_ref),
             (fraction_hbm, fraction_ref))
        )
    ]
    for fetch in fetches:
        fetch.start()
    cols = image_ref.shape[3]
    greeters = (
        has_up.astype(jnp.int32) + has_down.astype(jnp.int32) + (me != root).astype(jnp.int32)
    )
    pl.semaphore_wait(barrier, greeters)

    @pl.when(me != root)
    def _():
        pl.semaphore_signal(join_sem, inc=1, device_id={"acq": root}, device_id_type=MESH)

    to_down = pltpu.make_async_remote_copy(
        src_ref=image_hbm.at[:, ROWS - ABOVE :], dst_ref=halo_top,
        send_sem=halo_send_sem.at[0], recv_sem=halo_recv_sem.at[0],
        device_id={"band": down}, device_id_type=MESH,
    )
    to_up = pltpu.make_async_remote_copy(
        src_ref=image_hbm.at[:, :BELOW], dst_ref=halo_bottom,
        send_sem=halo_send_sem.at[1], recv_sem=halo_recv_sem.at[1],
        device_id={"band": up}, device_id_type=MESH,
    )

    @pl.when(has_down)
    def _():
        to_down.start()

    @pl.when(has_up)
    def _():
        to_up.start()

    @pl.when(jnp.logical_not(has_up))
    def _():
        halo_top[...] = jnp.zeros_like(halo_top)

    @pl.when(jnp.logical_not(has_down))
    def _():
        halo_bottom[...] = jnp.zeros_like(halo_bottom)

    offsets[...] = jnp.zeros_like(offsets)
    for fetch in fetches:
        fetch.wait()
    offsets[0, :2, :acqs] = shift_ref[...]
    offsets[1, :2, :acqs] = fraction_ref[...]
    lane = lax.broadcasted_iota(jnp.int32, (8, 128), 1)
    sub = lax.broadcasted_iota(jnp.int32, (8, 128), 0)

    held = (jnp.where(sub < acqs, sub, sub - 2), sub & 3)
    held_part = (jnp.where(sub < acqs, 0.0, 1.0), jnp.ones((8, 128), f32))

    def offset_weights(which, group):
        shift, fraction = (
            jnp.sum(
                jnp.where(lane == held[group], offsets[i, which : which + 1, :], 0),
                axis=1, keepdims=True,
            )
            for i in range(2)
        )
        taps = jnp.where((lane >> 3) == fraction, index_ref[8:9, :128], 0.0)
        for step in (8, 16, 32, 64):
            taps = taps + pltpu.roll(taps, step, 1)
        weights = []
        for off in range(1, 2 * HALO + 1):
            hit = (lane == off - (HALO - 3) - shift) & (lane < 8)
            weights.append(jnp.sum(jnp.where(hit, taps, 0.0), axis=1, keepdims=True))
        return weights

    row_weights = [offset_weights(0, group) for group in range(2)]
    col_weights = [offset_weights(1, group) for group in range(2)]

    def row_matrix(at):
        place = index_ref[at + 1 : at + 2, :]
        own = []
        for group in range(2):
            acq = jnp.concatenate([held[group].astype(f32)] * 2, axis=1)
            part = jnp.concatenate([held_part[group]] * 2, axis=1)
            own.append((index_ref[at : at + 1, :] == acq) & (index_ref[at + 2 : at + 3, :] == part))
        for r in range(ROWS):
            totals = [jnp.zeros((8, 256), f32)] * 2
            for off in range(1, 2 * HALO + 1):
                hit = place == float(off - HALO + r)
                for group in range(2):
                    totals[group] = jnp.where(hit, row_weights[group][off - 1], totals[group])
            for group in range(2):
                m = (r * 2 + group) * 8
                weight_ref[m : m + 8, :] = jnp.where(own[group], totals[group], 0.0)
        whole = weight_ref[...]
        high = whole.astype(bf16)
        low = (whole - high.astype(f32)).astype(bf16)
        return high, low

    def filtered(matrix, rows_ref, at):
        count = rows_ref.shape[0] * rows_ref.shape[1] * 2
        rows = rows_ref[...].reshape(count, cols)
        high, low = (half[:, at : at + count] for half in matrix)
        return jnp.dot(high, rows, preferred_element_type=f32) + jnp.dot(
            low, rows, preferred_element_type=f32
        )

    y_ref[:, LANES - 128 :] = jnp.zeros((ROWS * 16, 128), f32)
    y_ref[:, :cols] = filtered(row_matrix(2), image_ref, 0)
    matrix = row_matrix(5)

    def bits(v):
        place = lax.broadcasted_iota(jnp.int32, (16, 128), 1).astype(f32) + (128.0 * v + 0.5)
        rest = jnp.floor(place * (1.0 / PATCH))
        rest = rest - 16.0 * jnp.floor(rest * (1.0 / 16))
        found = []
        for bit in (8.0, 4.0, 2.0, 1.0):
            hit = jnp.where(rest >= bit, 1.0, 0.0)
            rest = rest - bit * hit
            found.append(hit.astype(bf16))
        return found[::-1]

    for v in range(WIDE // 128):
        for k, hit in enumerate(bits(v)):
            bit_ref[v, k] = hit

    @pl.when(has_up)
    def _():
        to_down.wait_recv()

    @pl.when(has_down)
    def _():
        to_up.wait_recv()

    y_ref[:, :cols] += filtered(matrix, halo_top, 0) + filtered(matrix, halo_bottom, 128)

    for r in range(ROWS):
        parts = []
        for group in range(2):
            m = (r * 2 + group) * 8
            y = y_ref[m : m + 8, :]
            moved = [y] + [pltpu.roll(y, LANES - low, 1) for low in range(1, 4)]
            z = None
            for high in range(4):
                total = None
                for low in range(4):
                    off = 4 * high + low
                    if 1 <= off <= 2 * HALO:
                        term = col_weights[group][off - 1] * moved[low]
                        total = term if total is None else total + term
                if 4 * high != 8:
                    total = pltpu.roll(total, (8 - 4 * high) % LANES, 1)
                z = total if z is None else z + total
            z = jnp.concatenate([z, jnp.zeros((8, WIDE - LANES), f32)], axis=1)
            parts.append(pltpu.roll(z, (PATCH * r + WIDE - 1) % WIDE, 1))
        z_ref[r] = jnp.concatenate(parts, axis=0).astype(bf16)

    for v in range(WIDE // 128):
        rows = [z_ref[r, :, 128 * v : 128 * v + 128] for r in range(ROWS)]
        rows = rows + rows[: 16 - ROWS]
        for k in range(4):
            hit = bit_ref[v, k] > 0.5
            rows = [jnp.where(hit, rows[(i + (1 << k)) % 16], rows[i]) for i in range(16)]
        for i in range(16):
            moved_ref[v, i] = rows[i]

    narrow = lax.broadcasted_iota(jnp.int32, (16, 128), 1).astype(f32).astype(bf16)
    upper = lax.broadcasted_iota(jnp.int32, (16, 128), 0).astype(f32).astype(bf16) < 12.0
    for j in range(peers):
        halves = []
        for q in (2 * j, 2 * j + 1):
            v = PATCH * q // 128
            value = moved_ref[v, -q % 16]
            if PATCH * q + PATCH * ROWS > 128 * (v + 1):
                value = jnp.where(
                    narrow >= float(PATCH * q - 128 * v), value, moved_ref[v + 1, -q % 16]
                )
            halves.append(value)
        send[j, 0:8, :] = halves[0][:8]
        send[j, 8:16, :] = halves[1][:8]
        send[j, 16:24, :] = jnp.where(upper, halves[0], halves[1])[8:]

    recv[me] = send[me]

    ys = [lax.rem(me // 8 + d, 4) * 8 for d in range(4)]
    xs = [lax.rem(lax.rem(me // 2, 4) + d, 4) * 2 for d in range(4)]
    cores = [lax.rem(me, 2), 1 - lax.rem(me, 2)]
    moves = sorted(
        ((dy, dx, dc) for dy in range(4) for dx in range(4) for dc in range(2) if dy or dx or dc),
        key=lambda move: -(4 * min(move[0], 4 - move[0]) + 2 * min(move[1], 4 - move[1]) + move[2]),
    )
    targets = [ys[dy] + xs[dx] + cores[dc] for dy, dx, dc in moves]
    sources = [ys[-dy] + xs[-dx] + cores[dc] for dy, dx, dc in moves]

    def block_copy(src, dst):
        return pltpu.make_async_remote_copy(
            src_ref=send.at[dst], dst_ref=recv.at[src],
            send_sem=send_sem.at[dst], recv_sem=recv_sem.at[src],
            device_id={"acq": dst}, device_id_type=MESH,
        )

    @pl.when(me == root)
    def _():
        pl.semaphore_wait(join_sem, peers - 1)
        lax.fori_loop(1, peers, let_go, 0)

    @pl.when(me != root)
    def _():
        pl.semaphore_wait(go_sem, 1)

    blocks_out = [block_copy(me, dst) for dst in targets]
    blocks_in = [block_copy(src, src) for src in sources]
    for copy in blocks_out:
        copy.start()

    count = peers * 8
    used = []
    for p in range(2):
        spot = lax.rem(lane + (128 * peers - PATCH * p) - 2 * PATCH * me, 128)
        used.append((spot < PATCH * ROWS) & (sub < acqs))
    order = [me] + sources[::-1]
    waits = [None] + blocks_in[::-1]
    diagonals = [[jnp.zeros((8, 128), f32)] * (count // 128) for p in range(2)]
    for first, last in ((0, peers - 8), (peers - 8, peers)):
        straight, crossed = [[], []], [[], []]
        for k in range(first, last):
            if waits[k] is not None:
                waits[k].wait_recv()
        for k in range(first, last):
            block = recv[order[k]].astype(f32)
            near, far, rest = block[:8], block[8:16], block[16:]
            for p, (re, im, late) in enumerate(
                ((near, rest, near), (far, pltpu.roll(rest, 4, 0), far))
            ):
                im = jnp.where(sub < 4, im, pltpu.roll(late, 6, 0))
                re, im = jnp.where(used[p], re, 0.0), jnp.where(used[p], im, 0.0)
                power = jnp.sum(re * re + im * im, axis=1, keepdims=True) / (PATCH * PATCH) + 1e-06
                scale = jnp.broadcast_to(lax.rsqrt(power) / PATCH, (8, 128))
                column[p, 0, 8 * k : 8 * k + 8, :] = scale
                half, at = 8 * k // 128, 8 * k % 128
                diagonals[p][half] = jnp.where(lane == sub + at, scale, diagonals[p][half])
                straight[p].append(jnp.concatenate([re, im], axis=1))
                crossed[p].append(jnp.concatenate([im, -re], axis=1))
        for p in range(2):
            lhs_ref[p, 8 * first : 8 * last] = jnp.concatenate(straight[p], axis=0).astype(bf16)
            lhs_ref[p, count + 8 * first : count + 8 * last] = jnp.concatenate(
                crossed[p], axis=0
            ).astype(bf16)
    for p in range(2):
        gram[2 * count * p : 2 * count * (p + 1)] = lax.dot_general(
            lhs_ref[p], lhs_ref[p, :count], (((1,), (1,)), ((), ())), preferred_element_type=f32
        )

    groups = peers
    norm = 2.0 * peers * acqs
    both = (0, 1)

    def load(p, part, at):
        return gram[pl.ds((2 * p + part) * count + at, 8), :]

    def twice(value):
        return jnp.concatenate([value] * (count // 128), axis=1)

    scale_rows = [
        jnp.sum(jnp.concatenate(halves, axis=1), axis=0, keepdims=True) for halves in diagonals
    ]

    def by_columns(g, totals, first):
        at = pl.multiple_of(g * 8, 8)
        new = []
        for p in both:
            tr, ti = totals[p]
            gr, gi = load(p, 0, at), load(p, 1, at)
            if first:
                scale = twice(column[p, 0, pl.ds(at, 8), :])
                new.append((tr + gr * scale, ti - gi * scale))
            else:
                ur = twice(column[p, 1, pl.ds(at, 8), :])
                ui = twice(column[p, 2, pl.ds(at, 8), :])
                new.append((tr + (gr * ur + gi * ui), ti + (gr * ui - gi * ur)))
        return tuple(new)

    def by_rows(g, totals, vectors, last):
        at = pl.multiple_of(g * 8, 8)
        new = []
        for p in both:
            ur, ui = vectors[p]
            gr, gi = load(p, 0, at), load(p, 1, at)
            scale = column[p, 0, pl.ds(at, 8), :]
            wr = jnp.sum(gr * ur - gi * ui, axis=1, keepdims=True) * scale
            wi = jnp.sum(gr * ui + gi * ur, axis=1, keepdims=True) * scale
            column[p, 1, pl.ds(at, 8), :] = wr if last else wr * scale
            column[p, 2, pl.ds(at, 8), :] = wi if last else wi * scale
            new.append(totals[p] + (wr * wr + wi * wi))
        return tuple(new)

    inverses = [None, None]
    for step in range(0, ITERS, 2):
        zero = jnp.zeros((8, count), f32)
        totals = lax.fori_loop(
            0, groups, functools.partial(by_columns, first=step == 0), ((zero, zero),) * 2, unroll=32
        )
        vectors = []
        for p in both:
            scale = scale_rows[p] if step == 0 else scale_rows[p] * inverses[p][:, :1]
            wr = jnp.sum(totals[p][0], axis=0, keepdims=True) * scale
            wi = jnp.sum(totals[p][1], axis=0, keepdims=True) * scale
            power = jnp.sum(wr * wr + wi * wi, axis=1, keepdims=True)
            scale = lax.rsqrt(power / norm + 1e-06) * scale_rows[p]
            vectors.append(tuple(jnp.broadcast_to(w * scale, (8, count)) for w in (wr, wi)))
        totals = lax.fori_loop(
            0, groups, functools.partial(by_rows, vectors=vectors, last=step + 2 == ITERS),
            (jnp.zeros((8, 128), f32),) * 2, unroll=32,
        )
        for p in both:
            power = jnp.sum(totals[p], axis=0, keepdims=True)
            inverses[p] = lax.rsqrt(power / norm + 1e-06)

    choice = lane >> 3
    factor = jnp.where((lane & 7) == sub, jnp.where(choice < 2, inverses[0], inverses[1]), 0.0)
    factor = jnp.where(choice < 4, factor, 0.0)

    def back_copy(src, dst, group):
        return pltpu.make_async_remote_copy(
            src_ref=back_send.at[group], dst_ref=back_recv.at[src],
            send_sem=back_send_sem.at[dst], recv_sem=back_recv_sem.at[src],
            device_id={"acq": dst}, device_id_type=MESH,
        )

    backs_out = [back_copy(me, order[g], g) for g in range(peers - 1, 0, -1)]
    backs_in = [back_copy(src, src, 0) for src in targets]
    for g in range(peers - 1, -1, -1):
        rows = slice(8 * g, 8 * g + 8)
        re = jnp.where(choice < 2, column[0, 1, rows, :], column[1, 1, rows, :])
        im = jnp.where(choice < 2, column[0, 2, rows, :], column[1, 2, rows, :])
        value = jnp.where((choice & 1) == 0, re, im) * factor
        back_send[g] = jnp.sum(value, axis=0, keepdims=True)
        if g:
            backs_out[peers - 1 - g].start()
    back_recv[me] = back_send[0]
    for copy in blocks_out:
        copy.wait_send()
    for copy in backs_in[::-1]:
        copy.wait_recv()

    values = back_recv[...].reshape(peers, 128)
    into = lax.broadcasted_iota(jnp.int32, (peers, 4 * peers), 1)
    source = lax.broadcasted_iota(jnp.int32, (peers, 4 * peers), 0)
    into = into - jnp.where(into < 2 * peers, 0, 2 * peers + 1)
    result = lax.dot_general(
        values[:, :32], (into == 2 * source).astype(f32),
        (((0,), (0,)), ((), ())), precision=lax.Precision.HIGHEST, preferred_element_type=f32,
    )
    result = result[:16, : 2 * peers] + pltpu.roll(result[16:], 2 * peers, 1)[:, : 2 * peers]
    for c in range(2):
        out_ref[c, :, 0, :] = result[8 * c : 8 * c + acqs]
    for copy in backs_out:
        copy.wait_send()

    @pl.when(has_down)
    def _():
        to_down.wait_send()

    @pl.when(has_up)
    def _():
        to_up.wait_send()


def on_device(images, pixel_shift, fraction_index):
    acqs = images.shape[1]
    peers = lax.axis_size("acq")
    bands = lax.axis_size("band")
    f32, bf16 = jnp.float32, jnp.bfloat16
    vmem = pl.BlockSpec(memory_space=pltpu.VMEM)
    dma = pltpu.SemaphoreType.DMA
    return pl.pallas_call(
        functools.partial(kernel, acqs, peers, bands),
        out_shape=pltpu.VMEM((2, acqs, 1, 2 * peers), f32),
        in_specs=[pl.BlockSpec(memory_space=pl.ANY)] * 4,
        out_specs=vmem,
        scratch_shapes=[
            pltpu.VMEM((2, acqs), jnp.int32),
            pltpu.VMEM((2, acqs), jnp.int32),
            pltpu.VMEM((16, 256), f32),
            pltpu.VMEM((acqs, ROWS, 2, images.shape[3]), bf16),
            pltpu.VMEM((2, 8, 128), jnp.int32),
            pltpu.VMEM((acqs, ABOVE, 2, images.shape[3]), bf16),
            pltpu.VMEM((acqs, BELOW, 2, images.shape[3]), bf16),
            pltpu.VMEM((2 * ROWS * 8, 256), f32),
            pltpu.VMEM((2 * ROWS * 8, LANES), f32),
            pltpu.VMEM((ROWS, 16, WIDE), bf16),
            pltpu.VMEM((WIDE // 128, 16, 16, 128), bf16),
            pltpu.VMEM((WIDE // 128, 4, 16, 128), bf16),
            pltpu.VMEM((peers, 24, 128), bf16),
            pltpu.VMEM((peers, 24, 128), bf16),
            pltpu.VMEM((2, 2 * peers * 8, 256), bf16),
            pltpu.VMEM((4 * peers * 8, peers * 8), f32),
            pltpu.VMEM((2, 3, peers * 8, 128), f32),
            pltpu.VMEM((peers, 1, 128), f32),
            pltpu.VMEM((peers, 1, 128), f32),
            dma((4,)), pltpu.SemaphoreType.REGULAR, pltpu.SemaphoreType.REGULAR,
            dma((2,)), dma((2,)),
            dma((peers,)), dma((peers,)),
            dma((peers,)), dma((peers,)),
        ],
        compiler_params=pltpu.CompilerParams(
            collective_id=0, has_side_effects=True, vmem_limit_bytes=60 * 1024 * 1024
        ),
    )(*(
        pltpu.with_memory_space_constraint(operand, pltpu.HBM)
        for operand in (
            pixel_shift.T, fraction_index.T, jnp.asarray(index_rows(acqs)),
            jnp.transpose(images, (1, 2, 0, 3)),
        )
    ))


def solution(mesh):
    placed = (P(None, "acq", "band", None), P("acq", None), P("acq", None))
    return jax.shard_map(
        on_device,
        mesh=mesh,
        in_specs=placed,
        out_specs=P(None, "acq", "band", None),
        check_vma=False,
    )
```
